1024 devices in a mesh: sample: 16 (over z_lo, core), depth: 16 (over y, z_hi), height: 4 (over x).
Axes of the slice: x: 4, y: 4, z: 32 (z_hi: 4, z_lo: 8; z = z_hi * 8 + z_lo), core: 2. Of those that a mesh axis runs over, the one named last changes fastest.
Arguments:
- volume: bfloat16 [256, 16, 16, 16, 128], P('sample', 'depth', 'height'), may hold values from -6 to 6
- conv_weight: bfloat16 [3456, 256], replicated, may hold values from -0.109375 to 0.109375
- dense_weight: bfloat16 [16, 4, 1024, 128], P('depth', 'height'), may hold values from -0.09375 to 0.09375
- mid_weight: float32 [128, 64], replicated, may hold values from -0.5 to 0.5
- out_weight: float32 [64, 4], replicated, may hold values from -0.75 to 0.75
- targets: float32 [256, 4], P('sample'), may hold values from -4 to 4
Outputs:
- predictions: float32 [256, 4], P('sample')
- dense_grad: float32 [16, 4, 1024, 128], P('depth', 'height')
- conv_grad: float32 [3456, 256], P(('depth', 'height'), 'sample')
The draws below stay inside these ranges and needn't reach their ends.
All inputs are finite; a program needn't handle non-finite values.
Results may differ from the reference program's by a relative error of at most 0.0051.
Values may be sent and summed in bfloat16 or wider, within the bound.
A program may use at most 64 MiB of HBM per device.

```python
import jax
import jax.numpy as jnp
from jax import lax

C_IN = 128
C_OUT = 256
HID = 128
HID2 = 64
NOUT = 4
VW = 16
SAMPLES = 256
VD = 16
VH = 16


def level_of(stream_key, dims, shards, smallest, high):
    def one(axis_at, blocks):
        heights = jax.random.uniform(jax.random.fold_in(jax.random.fold_in(stream_key, 6), axis_at), (blocks,), jnp.float32, smallest / len(shards), high / len(shards))
        return jnp.repeat(jnp.exp(heights), dims[axis_at] // blocks).reshape((-1,) + (1,) * (len(dims) - axis_at - 1))

    level = one(*shards[0])
    for cut in shards[1:]:
        level = level * one(*cut)
    return level


def scatter_about(key, shape, scale, most, cuts=(), kind=jnp.bfloat16):
    gain = level_of(key, shape, cuts, -0.22, 0.18) if cuts else 1.0
    values = jax.random.normal(key, shape, jnp.float32) * scale * gain
    return jnp.minimum(jnp.maximum(values, -most), most).astype(kind)


def setup_inputs(seed: int = 0) -> dict:
    arg_keys = jax.random.split(jax.random.key(seed), 7)
    return {
        "volume": scatter_about(arg_keys[0], (SAMPLES, VD, VH, VW, C_IN), 1.0, 6.0, ((0, 16), (1, 16), (2, 4))),
        "conv_weight": scatter_about(arg_keys[1], (27 * C_IN, C_OUT), (27 * C_IN) ** -0.5, 0.109375),
        "dense_weight": scatter_about(arg_keys[2], (VD, VH // 4, (VW // 4) * C_OUT, HID), (VD * (VH // 4) * (VW // 4) * C_OUT // 16) ** -0.5, 0.09375, ((0, 16), (1, 4))),
        "mid_weight": scatter_about(arg_keys[3], (HID, HID2), HID ** -0.5, 0.5, (), jnp.float32),
        "out_weight": scatter_about(arg_keys[4], (HID2, NOUT), HID2 ** -0.5, 0.75, (), jnp.float32),
        "targets": scatter_about(arg_keys[5], (SAMPLES, NOUT), 1.0, 4.0, ((0, 16),), jnp.float32),
    }


def gelu_slope(value):
    return jax.vjp(lambda v: jax.nn.gelu(v, approximate=True), value)[1](jnp.ones_like(value))[0]

def make_patches(padded, deep, high, wide):
    pieces = []
    for a in range(3):
        for b in range(3):
            for c in range(3):
                pieces.append(padded[a:a + deep, b:b + high, c:c + wide])
    return jnp.concatenate(pieces, axis=-1)

def sample_patches(single):
    padded = jnp.pad(single, ((1, 1), (1, 1), (1, 1), (0, 0)))
    return make_patches(padded, VD, VH, VW).reshape(VD * VH * VW, 27 * C_IN)

def pool_cells(active):
    blocks = active.reshape(VD, VH // 4, 4, VW // 4, 4, C_OUT)
    return lax.optimization_barrier(jnp.mean(blocks, axis=(2, 4))).reshape(VD, VH // 4, VW // 4 * C_OUT)

def reference(volume, conv_weight, dense_weight, mid_weight, out_weight, targets):
    hi = lax.Precision.HIGHEST

    def forward_one(single):
        pre = jnp.dot(sample_patches(single), conv_weight, preferred_element_type=jnp.float32)
        active = jax.nn.gelu(pre, approximate=True).reshape(VD, VH, VW, C_OUT)
        return pool_cells(active).astype(jnp.bfloat16)
    pooled = lax.map(forward_one, volume)
    flat = pooled.reshape(SAMPLES, -1)
    dense_flat = dense_weight.reshape(-1, HID)
    first = jnp.dot(flat, dense_flat, preferred_element_type=jnp.float32)
    second = jnp.dot(jax.nn.gelu(first, approximate=True), mid_weight, precision=hi)
    predictions = jnp.dot(jax.nn.gelu(second, approximate=True), out_weight, precision=hi)
    slope2 = gelu_slope(second) * jnp.dot(predictions - targets, out_weight.T, precision=hi)
    slope1 = (gelu_slope(first) * jnp.dot(slope2, mid_weight.T, precision=hi)).astype(jnp.bfloat16)
    dense_grad = jnp.dot(flat.T, slope1, preferred_element_type=jnp.float32).reshape(dense_weight.shape)
    back = jnp.dot(slope1, dense_flat.T, preferred_element_type=jnp.float32)

    def backward_one(total, pair):
        single, back_one = pair
        cells = sample_patches(single)
        pre = jnp.dot(cells, conv_weight, preferred_element_type=jnp.float32)
        spread = back_one.reshape(VD, VH // 4, 1, VW // 4, 1, C_OUT) / 16.0
        spread = jnp.broadcast_to(spread, (VD, VH // 4, 4, VW // 4, 4, C_OUT)).reshape(VD * VH * VW, C_OUT)
        cell_slope = (spread * gelu_slope(pre)).astype(jnp.bfloat16)
        return (total + jnp.dot(cells.T, cell_slope, preferred_element_type=jnp.float32), None)
    start = jnp.zeros((27 * C_IN, C_OUT), jnp.float32)
    conv_grad, _ = lax.scan(backward_one, start, (volume, back))
    return (predictions, dense_grad, conv_grad)
```

```python
import jax
import jax.numpy as jnp
from jax import lax
from jax.experimental import pallas as pl
from jax.experimental.pallas import tpu as pltpu
from jax.sharding import PartitionSpec as P

F32 = jnp.float32
BF16 = jnp.bfloat16
MESH = pl.DeviceIdType.MESH


def place():
    sample, depth, x = lax.axis_index("sample"), lax.axis_index("depth"), lax.axis_index("height")
    return sample // 2, sample % 2, depth // 4, depth % 4, x


def partner(kind, step):
    z_lo, core, y, z_hi, x = place()
    if kind == "z_lo":
        z_lo = (z_lo + step) % 8
    elif kind == "core":
        core = (core + step) % 2
    elif kind == "y":
        y = (y + step) % 4
    elif kind == "z_hi":
        z_hi = (z_hi + step) % 4
    else:
        x = (x + step) % 4
    return (z_lo * 2 + core, y * 4 + z_hi, x)


def greet(partners):
    barrier = pltpu.get_barrier_semaphore()
    for kind, step in partners:
        pl.semaphore_signal(barrier, inc=1, device_id=partner(kind, step), device_id_type=MESH)


def met(partners):
    pl.semaphore_wait(pltpu.get_barrier_semaphore(), len(partners))


QUADS = [(kind, step) for kind in ("x", "y", "z_hi") for step in (1, 2, 3)]
OCTETS = [("z_lo", step) for step in range(1, 8)]


def first_kernel(part_ref, first_ref, held, send_sem, recv_sem):
    z_lo, core, y, z_hi, x = place()
    greet(QUADS)
    met(QUADS)
    total = part_ref[...]
    for stage, (kind, mine) in enumerate((("x", x), ("y", y), ("z_hi", z_hi))):
        held[stage, mine] = total
        copies = []
        for step in (1, 2, 3):
            at = stage * 3 + step - 1
            copy = pltpu.make_async_remote_copy(
                src_ref=held.at[stage, mine],
                dst_ref=held.at[stage, mine],
                send_sem=send_sem.at[at],
                recv_sem=recv_sem.at[at],
                device_id=partner(kind, step),
                device_id_type=MESH,
            )
            copy.start()
            copies.append(copy)
        for copy in copies:
            copy.wait()
        total = (held[stage, 0] + held[stage, 1]) + (held[stage, 2] + held[stage, 3])
    first_ref[...] = total


def sum_first(part):
    return pl.pallas_call(
        first_kernel,
        name="sum_first",
        out_shape=jax.ShapeDtypeStruct(part.shape, F32),
        in_specs=[pl.BlockSpec(memory_space=pltpu.VMEM)],
        out_specs=pl.BlockSpec(memory_space=pltpu.VMEM),
        scratch_shapes=[
            pltpu.VMEM((3, 4) + part.shape, F32),
            pltpu.SemaphoreType.DMA((9,)),
            pltpu.SemaphoreType.DMA((9,)),
        ],
        compiler_params=pltpu.CompilerParams(collective_id=0, has_side_effects=True),
    )(part)


GRAD_PARTNERS = [("core", 1)] + QUADS + OCTETS


def grads_kernel(
    kern_ref, pooled_ref, slope_ref, dense_ref, conv_ref,
    core_in, y_out, y_in, y_sum, x_out, x_in, lo_out, lo_in, hi_out, hi_in,
    feat, feat_pair, slopes, slopes_pair, piece, pieces, pieces_pair,
    send_sem, recv_sem,
):
    z_lo, core, y, z_hi, x = place()
    used = [0]

    def copy_to(kind, step, src, dst):
        at = used[0]
        used[0] += 1
        copy = pltpu.make_async_remote_copy(
            src_ref=src, dst_ref=dst, send_sem=send_sem.at[at], recv_sem=recv_sem.at[at],
            device_id=partner(kind, step), device_id_type=MESH,
        )
        copy.start()
        return copy

    greet(GRAD_PARTNERS)
    met(GRAD_PARTNERS)
    mine = pl.ds(pl.multiple_of(core * 128, 128), 128)
    theirs = pl.ds(pl.multiple_of(128 - core * 128, 128), 128)
    core_copies = []
    for step in (1, 2, 3, 0):
        to = (y + step) % 4
        core_copies.append(
            copy_to("core", 1, kern_ref.at[to, :, theirs], core_in.at[to])
        )
    feat[z_lo] = pooled_ref[:, pl.ds(pl.multiple_of(z_lo * 128, 128), 128)]
    slopes[z_lo] = slope_ref[...]
    lo_copies = []
    for kind, step in OCTETS:
        to = (z_lo + step) % 8
        lo_copies.append(
            copy_to(kind, step, pooled_ref.at[:, pl.ds(pl.multiple_of(to * 128, 128), 128)], feat.at[z_lo])
        )
        lo_copies.append(copy_to(kind, step, slope_ref, slopes.at[z_lo]))
    y_copies = []
    for turn, step in enumerate((1, 2, 3, 0)):
        to = (y + step) % 4
        core_copies[turn].wait_recv()
        total = kern_ref[to, :, mine].astype(F32) + core_in[to].astype(F32)
        if step:
            y_out[step - 1] = total.astype(BF16)
            y_copies.append(copy_to("y", step, y_out.at[step - 1], y_in.at[step - 1]))
        else:
            y_sum[0:864] = total
    y_sum[864:896] = jnp.zeros((32, 128), F32)
    for copy in lo_copies:
        copy.wait()
    pair = [copy_to("core", 1, feat, feat_pair), copy_to("core", 1, slopes, slopes_pair)]
    for copy in pair:
        copy.wait()
    over = (((0,), (0,)), ((), ()))
    grad = lax.dot_general(
        feat[...].reshape(128, 128), slopes[...].reshape(128, 128), over, preferred_element_type=F32
    ) + lax.dot_general(
        feat_pair[...].reshape(128, 128), slopes_pair[...].reshape(128, 128), over, preferred_element_type=F32
    )
    piece[...] = grad
    own = piece[pl.ds(pl.multiple_of(core * 64, 64), 64)].astype(BF16)
    pieces[z_lo] = own
    piece_copies = [copy_to(kind, step, pieces.at[z_lo], pieces.at[z_lo]) for kind, step in OCTETS]
    for copy in y_copies:
        copy.wait()
    y_sum[0:864] = (y_sum[0:864] + y_in[0].astype(F32)) + (y_in[1].astype(F32) + y_in[2].astype(F32))
    for hi in range(4):
        for to in range(4):
            start = (hi * 4 + to) * 54
            x_out[to, hi] = y_sum[start : start + 64].astype(BF16)
    x_copies = []
    for step in (1, 2, 3):
        x_copies.append(copy_to("x", step, x_out.at[(x + step) % 4], x_in.at[step - 1]))
    for copy in x_copies:
        copy.wait()
    blocks = (x_out[x].astype(F32) + x_in[0].astype(F32)) + (x_in[1].astype(F32) + x_in[2].astype(F32))
    for half in range(2):
        both = jnp.concatenate([blocks[2 * half].T, blocks[2 * half + 1].T], axis=1)
        lo_out[:, half] = both.reshape(8, 16, 128).astype(BF16)
    turn_copies = []
    for kind, step in OCTETS:
        turn_copies.append(copy_to(kind, step, lo_out.at[(z_lo + step) % 8], lo_in.at[step - 1]))
    for copy in turn_copies:
        copy.wait()
    total = lo_out[z_lo].astype(F32)
    for step in range(7):
        total = total + lo_in[step].astype(F32)
    hi_out[...] = total
    hi_copies = []
    for step in (1, 2, 3):
        hi_copies.append(copy_to("z_hi", step, hi_out.at[((z_hi + step) % 4) // 2], hi_in.at[step - 1]))
    for copy in piece_copies:
        copy.wait()
    last = copy_to("core", 1, pieces, pieces_pair)
    last.wait()
    for at in range(8):
        dense_ref[pl.ds(pl.multiple_of(at * 128 + core * 64, 64), 64)] = pieces[at].astype(F32)
        dense_ref[pl.ds(pl.multiple_of(at * 128 + 64 - core * 64, 64), 64)] = pieces_pair[at].astype(F32)
    for copy in hi_copies:
        copy.wait()
    total = (hi_out[z_hi // 2] + hi_in[0]) + (hi_in[1] + hi_in[2])
    turned = total.T
    conv_ref[...] = jnp.where(z_hi % 2 == 0, turned[0:54], turned[64:118])
    for copy in core_copies:
        copy.wait_send()


def sum_grads(kern, pooled, slope1):
    any_vmem = pl.BlockSpec(memory_space=pltpu.VMEM)
    copies = 4 + 14 + 3 + 2 + 7 + 3 + 7 + 3 + 1
    return pl.pallas_call(
        grads_kernel,
        name="sum_grads",
        out_shape=(
            jax.ShapeDtypeStruct((1024, 128), F32),
            jax.ShapeDtypeStruct((54, 16), F32),
        ),
        in_specs=[any_vmem] * 3,
        out_specs=(any_vmem, any_vmem),
        scratch_shapes=[
            pltpu.VMEM((4, 864, 128), BF16),
            pltpu.VMEM((3, 864, 128), BF16),
            pltpu.VMEM((3, 864, 128), BF16),
            pltpu.VMEM((896, 128), F32),
            pltpu.VMEM((4, 4, 64, 128), BF16),
            pltpu.VMEM((3, 4, 64, 128), BF16),
            pltpu.VMEM((8, 2, 16, 128), BF16),
            pltpu.VMEM((7, 2, 16, 128), BF16),
            pltpu.VMEM((2, 16, 128), F32),
            pltpu.VMEM((3, 16, 128), F32),
            pltpu.VMEM((8, 16, 128), BF16),
            pltpu.VMEM((8, 16, 128), BF16),
            pltpu.VMEM((8, 16, 128), BF16),
            pltpu.VMEM((8, 16, 128), BF16),
            pltpu.VMEM((128, 128), F32),
            pltpu.VMEM((8, 64, 128), BF16),
            pltpu.VMEM((8, 64, 128), BF16),
            pltpu.SemaphoreType.DMA((copies,)),
            pltpu.SemaphoreType.DMA((copies,)),
        ],
        compiler_params=pltpu.CompilerParams(
            collective_id=1, has_side_effects=True, vmem_limit_bytes=40 * 2**20
        ),
    )(kern, pooled, slope1)


def padded_2(cells, sides, width):
    for axis, dim in sides:
        count = lax.axis_size(axis)
        ends = count - 1
        head = lax.slice_in_dim(cells, 0, width, axis=dim)
        tail = lax.slice_in_dim(cells, cells.shape[dim] - width, cells.shape[dim], axis=dim)
        cells = jnp.concatenate(
            [
                lax.ppermute(tail, axis, [(i, (i + 1) % count) for i in range(ends)]),
                cells,
                lax.ppermute(head, axis, [((i + 1) % count, i) for i in range(ends)]),
            ],
            axis=dim,
        )
    return cells


def gelu_slope(value):
    return jax.vjp(lambda v: jax.nn.gelu(v, approximate=True), value)[1](jnp.ones_like(value))[0]


def per_device(volume, conv_weight, dense_weight, mid_weight, out_weight, targets):
    hi = lax.Precision.HIGHEST
    samp, deep, high, wide, chans = volume.shape
    outs = conv_weight.shape[1]
    padded = padded_2(volume, (("depth", 1), ("height", 2)), 1)
    padded = jnp.pad(padded, ((0, 0), (0, 0), (0, 0), (1, 1), (0, 0)))
    pieces = []
    for a in range(3):
        for b in range(3):
            for c in range(3):
                pieces.append(padded[:, a : a + deep, b : b + high, c : c + wide])
    cells = jnp.concatenate(pieces, axis=-1).reshape(samp * deep * high * wide, 27 * chans)
    pre = jnp.dot(cells, conv_weight, preferred_element_type=jnp.float32)
    active = jax.nn.gelu(pre, approximate=True).reshape(
        samp, deep, high // 4, 4, wide // 4, 4, outs
    )
    pooled = jnp.mean(active, axis=(3, 5)).astype(jnp.bfloat16)
    flat = pooled.reshape(samp, -1)
    dense_flat = dense_weight.reshape(-1, dense_weight.shape[-1])
    partial_value = jnp.dot(flat, dense_flat, preferred_element_type=jnp.float32)
    first = sum_first(partial_value)
    second = jnp.dot(jax.nn.gelu(first, approximate=True), mid_weight, precision=hi)
    predictions = jnp.dot(jax.nn.gelu(second, approximate=True), out_weight, precision=hi)
    slope2 = gelu_slope(second) * jnp.dot(predictions - targets, out_weight.T, precision=hi)
    slope1 = (gelu_slope(first) * jnp.dot(slope2, mid_weight.T, precision=hi)).astype(jnp.bfloat16)
    back = jnp.dot(slope1, dense_flat.T, preferred_element_type=jnp.float32)
    spread = back.reshape(samp, deep, high // 4, 1, wide // 4, 1, outs) / 16.0
    spread = jnp.broadcast_to(spread, (samp, deep, high // 4, 4, wide // 4, 4, outs)).reshape(
        -1, outs
    )
    cell_slope = (spread * gelu_slope(pre)).astype(jnp.bfloat16)
    cell_slope = cell_slope.reshape(-1, 8, 2, 16).swapaxes(1, 2).reshape(-1, outs)
    local_kernel = jnp.dot(cells.T, cell_slope, preferred_element_type=jnp.float32)
    kern = local_kernel.astype(BF16).reshape(4, 864, outs)
    dense_grad, conv_grad = sum_grads(kern, flat, slope1)
    return (predictions, dense_grad.reshape(dense_weight.shape), conv_grad)


def solution(mesh):
    in_specs = (
        P("sample", "depth", "height", None, None),
        P(),
        P("depth", "height", None, None),
        P(),
        P(),
        P("sample", None),
    )
    out_specs = (
        P("sample", None),
        P("depth", "height", None, None),
        P(("depth", "height"), "sample"),
    )
    return jax.shard_map(
        per_device, mesh=mesh, in_specs=in_specs, out_specs=out_specs, check_vma=False
    )
```

```python
import jax
import jax.numpy as jnp
from jax import lax
from jax.experimental import pallas as pl
from jax.experimental.pallas import tpu as pltpu
from jax.sharding import PartitionSpec as P

F32 = jnp.float32
BF16 = jnp.bfloat16
MESH = pl.DeviceIdType.MESH
EXACT = lax.Precision.HIGHEST


def place():
    sample, depth, x = lax.axis_index("sample"), lax.axis_index("depth"), lax.axis_index("height")
    return sample // 2, sample % 2, depth // 4, depth % 4, x


def partner(kind, step):
    z_lo, core, y, z_hi, x = place()
    if kind == "z_lo":
        z_lo = (z_lo + step) % 8
    elif kind == "z_four":
        z_lo = (z_lo // 4) * 4 + (z_lo + step) % 4
    elif kind == "core":
        core = (core + step) % 2
    elif kind == "y":
        y = (y + step) % 4
    elif kind == "z_hi":
        z_hi = (z_hi + step) % 4
    else:
        x = (x + step) % 4
    return (z_lo * 2 + core, y * 4 + z_hi, x)


QUADS = [(kind, step) for kind in ("x", "y", "z_hi") for step in (1, 2, 3)]
OCTETS = [("z_lo", step) for step in range(1, 8)]
PARTNERS = [("core", 1)] + QUADS + OCTETS
COPIES = 128


def gelu_and_slope(value):
    rate = 0.7978845608028654
    square = value * value
    bend = jnp.tanh(rate * (value + 0.044715 * value * square))
    half = 0.5 * (1.0 + bend)
    slope = half + 0.5 * value * (1.0 - bend * bend) * (rate * (1.0 + 3 * 0.044715 * square))
    return value * half, slope


def one_hot(shape, test, kind, weight=1.0):
    row = lax.broadcasted_iota(jnp.int32, shape, 0)
    column = lax.broadcasted_iota(jnp.int32, shape, 1)
    return jnp.where(test(row, column), weight, 0.0).astype(kind)


def kernel(
    vol_ref, weight_ref, dense_w_ref, mid_ref, out_w_ref, targets_ref,
    pred_ref, dense_ref, conv_ref,
    ext, wide, slope_at, summed, pool, pool_out, gathered, held, back, turned, preds,
    kern, core_in, y_out, y_in, y_sum, x_out, x_in, lo_out, lo_in, hi_out, hi_in,
    feat, feat_pair, slopes, slopes_pair, part_out, part_in, pieces, pieces_pair,
    send_sem, recv_sem, local_sem,
):
    z_lo, core, y, z_hi, x = place()
    used = [0]

    def reserve(count):
        used[0] += count
        assert used[0] <= COPIES
        return used[0] - count

    def copy_to(kind, step, src, dst):
        at = reserve(1)
        copy = pltpu.make_async_remote_copy(
            src_ref=src, dst_ref=dst, send_sem=send_sem.at[at], recv_sem=recv_sem.at[at],
            device_id=partner(kind, step), device_id_type=MESH,
        )
        copy.start()
        return copy

    barrier = pltpu.get_barrier_semaphore()
    for kind, step in PARTNERS:
        pl.semaphore_signal(barrier, inc=1, device_id=partner(kind, step), device_id_type=MESH)
    own = pltpu.make_async_copy(vol_ref.at[pl.ds(z_hi * 4, 4)], ext.at[:, 1 + z_hi, 1:5], local_sem)
    own.start()
    own.wait()
    pl.semaphore_wait(barrier, len(PARTNERS))

    vol_copies = []
    for step in (2, 1, 3):
        to = (z_hi + step) % 4
        vol_copies.append(
            copy_to("z_hi", step, vol_ref.at[pl.ds(to * 4, 4)], ext.at[:, 1 + z_hi, 1:5])
        )
    share = pl.ds(pl.multiple_of(core * 512 + (z_lo % 4) * 128, 128), 128)
    hi_weights = [
        copy_to("z_hi", step, dense_w_ref.at[share], gathered.at[step - 1, share]) for step in (2, 1, 3)
    ]
    for copy in vol_copies:
        copy.wait_recv()
    y_halo = [
        copy_to("y", 1, ext.at[:, 4, 1:5], ext.at[:, 0, 1:5]),
        copy_to("y", 3, ext.at[:, 1, 1:5], ext.at[:, 5, 1:5]),
    ]
    x_halo = [
        copy_to("x", 1, ext.at[:, 1:5, 4], ext.at[:, 1:5, 0]),
        copy_to("x", 3, ext.at[:, 1:5, 1], ext.at[:, 1:5, 5]),
    ]
    for copy, at in zip(y_halo, (0, 5)):
        copy.wait_recv()
        x_halo.append(copy_to("x", 1, ext.at[:, at, 4], ext.at[:, at, 0]))
        x_halo.append(copy_to("x", 3, ext.at[:, at, 1], ext.at[:, at, 5]))
    for copy in hi_weights:
        copy.wait_recv()
    lo_weights = [
        copy_to("z_four", step, gathered.at[:, share], gathered.at[:, share]) for step in (1, 2, 3)
    ]
    for copy in x_halo:
        copy.wait()
    for copy in vol_copies + y_halo + hi_weights:
        copy.wait_send()

    @pl.when(y == 0)
    def _():
        ext[:, 0] = jnp.zeros((4, 6, 16, 128), BF16)

    @pl.when(y == 3)
    def _():
        ext[:, 5] = jnp.zeros((4, 6, 16, 128), BF16)

    @pl.when(x == 0)
    def _():
        ext[:, :, 0] = jnp.zeros((4, 6, 16, 128), BF16)

    @pl.when(x == 3)
    def _():
        ext[:, :, 5] = jnp.zeros((4, 6, 16, 128), BF16)

    def forward(s, carry):
        cells = ext[s].reshape(36, 16, 128).astype(F32)
        edge = jnp.zeros((36, 1, 128), F32)
        wide[s, :, :, :, 0:128] = (
            jnp.concatenate([edge, cells[:, :15]], axis=1).astype(BF16).reshape(6, 6, 16, 128)
        )
        wide[s, :, :, :, 128:256] = ext[s]
        wide[s, :, :, :, 256:384] = (
            jnp.concatenate([cells[:, 1:], edge], axis=1).astype(BF16).reshape(6, 6, 16, 128)
        )
        pre = jnp.zeros((256, 256), F32)
        for tap in range(9):
            a, b = tap // 3, tap % 3
            pre = pre + jnp.dot(
                wide[s, a : a + 4, b : b + 4].reshape(256, 384),
                weight_ref[tap * 384 : tap * 384 + 384],
                preferred_element_type=F32,
            )
        active, slope = gelu_and_slope(pre)
        slope_at[s] = slope
        summed[s] = jnp.sum(active.reshape(4, 4, 16, 256), axis=1).reshape(64, 256)
        return carry

    lax.fori_loop(0, 4, forward, 0)
    for copy in lo_weights:
        copy.wait()
    half_rows = pl.ds(pl.multiple_of(core * 512, 512), 512)
    pair_weights = copy_to("core", 1, gathered.at[:, half_rows], gathered.at[:, half_rows])

    spread = one_hot(
        (256, 256),
        lambda r, c: (r // 64 == c // 16 % 4)
        & (r // 16 % 4 == c % 16 // 4)
        & (r % 16 == z_hi * 4 + c // 64),
        F32,
        1.0 / 16,
    )
    pooled = jnp.dot(
        spread, summed[...].reshape(256, 256), precision=EXACT, preferred_element_type=F32
    ).astype(BF16)
    pool[...] = pooled.reshape(4, 4, 16, 256)
    order = one_hot(
        (64, 256),
        lambda r, c: (r // 16 == c // 16 % 4)
        & (r // 4 % 4 == c // 64)
        & (z_hi * 4 + r % 4 == c % 16),
        BF16,
    )
    pool_out[...] = (
        jnp.dot(order, pooled, preferred_element_type=F32).astype(BF16).reshape(4, 16, 256)
    )

    def features(at):
        return pool_out.at[at // 2, :, pl.ds(pl.multiple_of(at % 2 * 128, 128), 128)]

    feat_own = pltpu.make_async_copy(features(z_lo), feat.at[z_lo], local_sem)
    feat_own.start()
    feat_copies = [
        copy_to(kind, step, features((z_lo + step) % 8), feat.at[z_lo]) for kind, step in OCTETS
    ]
    feat_own.wait()
    total = jnp.zeros((16, 128), F32)
    for k in range(4):
        if k == 1:
            pair_weights.wait()
        for block in range(4):
            rows = slice(block * 256, block * 256 + 256)
            total = total + jnp.dot(
                pool[(z_hi - k + 4) % 4, block],
                dense_w_ref[rows] if k == 0 else gathered[k - 1, rows],
                preferred_element_type=F32,
            )
    for stage, (kind, mine) in enumerate((("x", x), ("y", y))):
        held[stage, mine] = total
        copies = [
            copy_to(kind, step, held.at[stage, mine], held.at[stage, mine]) for step in (1, 2, 3)
        ]
        for copy in copies:
            copy.wait()
        total = (held[stage, 0] + held[stage, 1]) + (held[stage, 2] + held[stage, 3])
    first = total
    out_w = jnp.concatenate([out_w_ref[...], jnp.zeros((64, 124), F32)], axis=1)
    targets = jnp.concatenate([targets_ref[...], jnp.zeros((16, 124), F32)], axis=1)
    across = (((1,), (1,)), ((), ()))
    first_gelu, first_slope = gelu_and_slope(first)
    second = jnp.dot(first_gelu, mid_ref[...], precision=EXACT, preferred_element_type=F32)
    second_gelu, second_slope = gelu_and_slope(second)
    pred = jnp.dot(second_gelu, out_w, precision=EXACT, preferred_element_type=F32)
    slope2 = second_slope * lax.dot_general(
        pred - targets, out_w, across, precision=EXACT, preferred_element_type=F32
    )
    slope1 = first_slope * lax.dot_general(
        slope2, mid_ref[...], across, precision=EXACT, preferred_element_type=F32
    )
    ours = lax.broadcasted_iota(jnp.int32, (16, 128), 0) // 4 == z_hi
    slope1 = jnp.where(ours, slope1, 0.0).astype(BF16)
    preds[z_hi] = jnp.where(ours, pred, 0.0)
    repeat = one_hot((16, 16), lambda r, c: z_hi * 4 + r % 4 == c, BF16)
    slopes[z_lo] = jnp.dot(repeat, slope1, preferred_element_type=F32).astype(BF16)
    slope_copies = [copy_to(kind, step, slopes.at[z_lo], slopes.at[z_lo]) for kind, step in OCTETS]
    pred_copies = [copy_to("z_hi", step, preds.at[z_hi], preds.at[z_hi]) for step in (1, 2, 3)]
    for k in range(4):
        for block in range(4):
            rows = slice(block * 256, block * 256 + 256)
            back[(z_hi - k + 4) % 4, block] = lax.dot_general(
                slope1, dense_w_ref[rows] if k == 0 else gathered[k - 1, rows], across,
                preferred_element_type=F32,
            )
    held_back = lax.dot_general(
        spread, back[...].reshape(256, 256), (((0,), (0,)), ((), ())), precision=EXACT,
        preferred_element_type=F32,
    )
    summed[...] = held_back.reshape(4, 64, 256)

    def turn(s, carry):
        spread_s = jnp.broadcast_to(summed[s].reshape(4, 1, 16, 256), (4, 4, 16, 256))
        cell = (spread_s.reshape(256, 256) * slope_at[s]).T.astype(BF16)
        for block in range(16):
            new = block % 2 * 8 + block // 2
            turned[s, new * 16 : new * 16 + 16] = cell[block * 16 : block * 16 + 16]
        return carry

    lax.fori_loop(0, 4, turn, 0)
    mine = pl.ds(pl.multiple_of(core * 128, 128), 128)
    theirs = pl.ds(pl.multiple_of(128 - core * 128, 128), 128)
    y_at = reserve(4)
    core_copies = []

    def y_copy(block, from_y):
        return pltpu.make_async_remote_copy(
            src_ref=y_out.at[block], dst_ref=y_in.at[from_y],
            send_sem=send_sem.at[y_at + block], recv_sem=recv_sem.at[y_at + from_y],
            device_id=partner("y", block - y + 4), device_id_type=MESH,
        )

    def over_y(block):
        core_copies[block].wait_recv()
        rows = slice(block * 864, block * 864 + 864)
        total = kern[rows, mine].astype(F32) + core_in[block].astype(F32)

        @pl.when(y == block)
        def _():
            y_sum[0:864] = total

        @pl.when(y != block)
        def _():
            y_out[block] = total.astype(BF16)
            y_copy(block, y).start()

    def grad_piece():
        for copy in feat_copies + slope_copies:
            copy.wait()
        return [copy_to("core", 1, feat, feat_pair), copy_to("core", 1, slopes, slopes_pair)]

    def grad_parts(pair):
        for copy in pair:
            copy.wait()
        over = (((0,), (0,)), ((), ()))
        slice_of = lax.broadcasted_iota(jnp.int32, (128, 128), 0) % 16 // 4

        def by_slice(ref):
            rows = ref[...].reshape(128, 128).astype(F32)
            return jnp.concatenate(
                [jnp.where(slice_of == d, rows, 0.0).astype(BF16) for d in range(4)], axis=1
            )

        grad = lax.dot_general(
            feat[...].reshape(128, 128), by_slice(slopes), over, preferred_element_type=F32
        ) + lax.dot_general(
            feat_pair[...].reshape(128, 128), by_slice(slopes_pair), over, preferred_element_type=F32
        )
        grad = jnp.where(core == 0, grad[0:64], grad[64:128])
        for d in range(4):
            part_out[d] = grad[:, d * 128 : d * 128 + 128].astype(BF16)
        return [
            copy_to("z_hi", step, part_out.at[(z_hi + step) % 4], part_in.at[step - 1])
            for step in (2, 1, 3)
        ]

    pair, part_copies = None, None
    for tap in range(9):
        a, b = tap // 3, tap % 3
        total = jnp.zeros((256, 384), F32)
        for s in range(4):
            total = total + jnp.dot(
                turned[s], wide[s, a : a + 4, b : b + 4].reshape(256, 384), preferred_element_type=F32
            )
        kern[tap * 384 : tap * 384 + 384] = total.T.astype(BF16)
        if tap in (2, 4, 6, 8):
            block = tap // 2 - 1
            rows = slice(block * 864, block * 864 + 864)
            core_copies.append(copy_to("core", 1, kern.at[rows, theirs], core_in.at[block]))
        if tap in (3, 5, 7):
            over_y(tap // 2 - 1)
        if tap == 7:
            pair = grad_piece()
    over_y(3)
    part_copies = grad_parts(pair)
    y_sum[864:896] = jnp.zeros((32, 128), F32)
    for block in range(4):

        @pl.when(y != block)
        def _(block=block):
            y_copy(block, block).wait()
            y_sum[0:864] = y_sum[0:864] + y_in[block].astype(F32)

    for hi in range(4):
        for to in range(4):
            start = (hi * 4 + to) * 54
            x_out[to, hi] = y_sum[start : start + 64].astype(BF16)
    x_copies = []
    for step in (1, 2, 3):
        x_copies.append(copy_to("x", step, x_out.at[(x + step) % 4], x_in.at[step - 1]))
    for copy in x_copies:
        copy.wait()
    blocks = (x_out[x].astype(F32) + x_in[0].astype(F32)) + (x_in[1].astype(F32) + x_in[2].astype(F32))
    for half in range(2):
        both = jnp.concatenate([blocks[2 * half].T, blocks[2 * half + 1].T], axis=1)
        lo_out[:, half] = both.reshape(8, 16, 128).astype(BF16)
    turn_copies = []
    for kind, step in OCTETS:
        turn_copies.append(copy_to(kind, step, lo_out.at[(z_lo + step) % 8], lo_in.at[step - 1]))
    for copy in turn_copies:
        copy.wait()
    total = lo_out[z_lo].astype(F32)
    for step in range(7):
        total = total + lo_in[step].astype(F32)
    hi_out[...] = total
    hi_copies = []
    for step in (2, 1, 3):
        hi_copies.append(copy_to("z_hi", step, hi_out.at[((z_hi + step) % 4) // 2], hi_in.at[step - 1]))
    for copy in part_copies:
        copy.wait()
    pieces[z_lo] = (
        (part_out[z_hi].astype(F32) + part_in[0].astype(F32))
        + (part_in[1].astype(F32) + part_in[2].astype(F32))
    ).astype(BF16)
    piece_copies = [copy_to(kind, step, pieces.at[z_lo], pieces.at[z_lo]) for kind, step in OCTETS]
    for copy in piece_copies:
        copy.wait()
    last = copy_to("core", 1, pieces, pieces_pair)
    for copy in pred_copies:
        copy.wait()
    pred_ref[...] = ((preds[0] + preds[1]) + (preds[2] + preds[3]))[:, 0:4]
    last.wait()
    for at in range(8):
        dense_ref[pl.ds(pl.multiple_of(at * 128 + core * 64, 64), 64)] = pieces[at].astype(F32)
        dense_ref[pl.ds(pl.multiple_of(at * 128 + 64 - core * 64, 64), 64)] = pieces_pair[at].astype(F32)
    for copy in hi_copies:
        copy.wait()
    total = (hi_out[z_hi // 2] + hi_in[0]) + (hi_in[1] + hi_in[2])
    across_rows = total.T
    conv_ref[...] = jnp.where(z_hi % 2 == 0, across_rows[0:54], across_rows[64:118])
    for copy in core_copies:
        copy.wait_send()


def per_device(volume, conv_weight, dense_weight, mid_weight, out_weight, targets):
    vmem = pl.BlockSpec(memory_space=pltpu.VMEM)
    predictions, dense_grad, conv_grad = pl.pallas_call(
        kernel,
        name="conv_and_head",
        out_shape=(
            jax.ShapeDtypeStruct((16, 4), F32),
            jax.ShapeDtypeStruct((1024, 128), F32),
            jax.ShapeDtypeStruct((54, 16), F32),
        ),
        in_specs=[vmem] * 6,
        out_specs=(vmem,) * 3,
        scratch_shapes=[
            pltpu.VMEM((4, 6, 6, 16, 128), BF16),
            pltpu.VMEM((4, 6, 6, 16, 384), BF16),
            pltpu.VMEM((4, 256, 256), F32),
            pltpu.VMEM((4, 64, 256), F32),
            pltpu.VMEM((4, 4, 16, 256), BF16),
            pltpu.VMEM((4, 16, 256), BF16),
            pltpu.VMEM((3, 1024, 128), BF16),
            pltpu.VMEM((2, 4, 16, 128), F32),
            pltpu.VMEM((4, 4, 16, 256), F32),
            pltpu.VMEM((4, 256, 256), BF16),
            pltpu.VMEM((4, 16, 128), F32),
            pltpu.VMEM((3456, 256), BF16),
            pltpu.VMEM((4, 864, 128), BF16),
            pltpu.VMEM((4, 864, 128), BF16),
            pltpu.VMEM((4, 864, 128), BF16),
            pltpu.VMEM((896, 128), F32),
            pltpu.VMEM((4, 4, 64, 128), BF16),
            pltpu.VMEM((3, 4, 64, 128), BF16),
            pltpu.VMEM((8, 2, 16, 128), BF16),
            pltpu.VMEM((7, 2, 16, 128), BF16),
            pltpu.VMEM((2, 16, 128), F32),
            pltpu.VMEM((3, 16, 128), F32),
            pltpu.VMEM((8, 16, 128), BF16),
            pltpu.VMEM((8, 16, 128), BF16),
            pltpu.VMEM((8, 16, 128), BF16),
            pltpu.VMEM((8, 16, 128), BF16),
            pltpu.VMEM((4, 64, 128), BF16),
            pltpu.VMEM((3, 64, 128), BF16),
            pltpu.VMEM((8, 64, 128), BF16),
            pltpu.VMEM((8, 64, 128), BF16),
            pltpu.SemaphoreType.DMA((COPIES,)),
            pltpu.SemaphoreType.DMA((COPIES,)),
            pltpu.SemaphoreType.DMA,
        ],
        compiler_params=pltpu.CompilerParams(
            collective_id=0, has_side_effects=True, vmem_limit_bytes=48 * 2**20
        ),
    )(
        volume.reshape(16, 4, 16, 128),
        conv_weight,
        dense_weight.reshape(1024, 128),
        mid_weight,
        out_weight,
        targets,
    )
    return predictions, dense_grad.reshape(dense_weight.shape), conv_grad


def solution(mesh):
    in_specs = (
        P("sample", "depth", "height", None, None),
        P(),
        P("depth", "height", None, None),
        P(),
        P(),
        P("sample", None),
    )
    out_specs = (
        P("sample", None),
        P("depth", "height", None, None),
        P(("depth", "height"), "sample"),
    )
    return jax.shard_map(
        per_device, mesh=mesh, in_specs=in_specs, out_specs=out_specs, check_vma=False
    )
```

```python
import jax
import jax.numpy as jnp
from jax import lax
from jax.experimental import pallas as pl
from jax.experimental.pallas import tpu as pltpu
from jax.sharding import PartitionSpec as P

F32 = jnp.float32
BF16 = jnp.bfloat16
MESH = pl.DeviceIdType.MESH
EXACT = lax.Precision.HIGHEST


def place():
    sample, depth, x = lax.axis_index("sample"), lax.axis_index("depth"), lax.axis_index("height")
    return sample // 2, sample % 2, depth // 4, depth % 4, x


def partner(kind, step):
    z_lo, core, y, z_hi, x = place()
    if kind == "z_lo":
        z_lo = (z_lo + step) % 8
    elif kind == "z_four":
        z_lo = (z_lo // 4) * 4 + (z_lo + step) % 4
    elif kind == "core":
        core = (core + step) % 2
    elif kind == "y":
        y = (y + step) % 4
    elif kind == "z_hi":
        z_hi = (z_hi + step) % 4
    elif kind == "x":
        x = (x + step) % 4
    else:
        y, x = (y + step[0]) % 4, (x + step[1]) % 4
    return (z_lo * 2 + core, y * 4 + z_hi, x)


QUADS = [(kind, step) for kind in ("x", "y", "z_hi") for step in (1, 2, 3)]
OTHERS = (2, 1, 3)
OCTET = range(1, 8)
CORNERS = [("corner", (dy, dx)) for dy in (1, 3) for dx in (1, 3)]
PARTNERS = [("core", 1)] + [q for q in QUADS if q != ("z_hi", 2)] + [("z_lo", step) for step in OCTET] + CORNERS
COPIES = 37


def gelu_and_slope(value):
    rate = 0.7978845608028654
    square = value * value
    bend = jnp.tanh(rate * (value + 0.044715 * value * square))
    half = 0.5 * (1.0 + bend)
    slope = half + 0.5 * value * (1.0 - bend * bend) * (rate * (1.0 + 3 * 0.044715 * square))
    return value * half, slope


def one_hot(shape, test, kind, weight=1.0):
    row = lax.broadcasted_iota(jnp.int32, shape, 0)
    column = lax.broadcasted_iota(jnp.int32, shape, 1)
    return jnp.where(test(row, column), weight, 0.0).astype(kind)


def kernel(
    vol_ref, weight_hbm, dense_w_hbm, mid_hbm, out_w_hbm, targets_hbm,
    pred_ref, dense_ref, conv_ref,
    weight_ref, dense_w_ref, mid_ref, out_w_ref, targets_ref,
    ext, wide, slope_at, summed, pool, pool_out, pool_in, vol_relay, gathered, held, back, turned, preds,
    kern, core_in, y_out, y_in, y_sum, x_out, x_in, lo_out, lo_in, hi_out, hi_in,
    feat, slopes, slope_in,
    send_sem, recv_sem, local_sem,
):
    z_lo, core, y, z_hi, x = place()
    used = [0]

    def reserve(count):
        used[0] += count
        assert used[0] <= COPIES
        return used[0] - count

    def copy_to(kind, step, src, dst):
        at = reserve(1)
        copy = pltpu.make_async_remote_copy(
            src_ref=src, dst_ref=dst, send_sem=send_sem.at[at], recv_sem=recv_sem.at[at],
            device_id=partner(kind, step), device_id_type=MESH,
        )
        copy.start()
        return copy

    def group_to(kind, steps, pair_of, span):
        at = reserve(1)
        sems = dict(send_sem=send_sem.at[at], recv_sem=recv_sem.at[at], device_id_type=MESH)
        for step in steps:
            src, dst = pair_of(step)
            pltpu.make_async_remote_copy(
                src_ref=src, dst_ref=dst, device_id=partner(kind, step), **sems
            ).start()
        return pltpu.make_async_remote_copy(
            src_ref=span, dst_ref=span, device_id=partner(kind, steps[0]), **sems
        )

    barrier = pltpu.get_barrier_semaphore()
    for kind, step in PARTNERS:
        pl.semaphore_signal(barrier, inc=1, device_id=partner(kind, step), device_id_type=MESH)
    local = [
        (vol_ref.at[pl.ds(z_hi * 4, 4)], ext.at[:, 1 + z_hi, 1:5]),
        (dense_w_hbm, dense_w_ref),
        (weight_hbm, weight_ref),
        (mid_hbm, mid_ref),
        (out_w_hbm, out_w_ref),
        (targets_hbm, targets_ref),
    ]
    local = [pltpu.make_async_copy(src, dst, local_sem.at[at]) for at, (src, dst) in enumerate(local)]
    for copy in local:
        copy.start()
    pl.semaphore_wait(barrier, len(PARTNERS))

    far = (z_hi + 2) % 4
    ways = ((0, 1), (1, 3))
    vol_on = [
        copy_to("z_hi", step, vol_ref.at[pl.ds(far * 4 + 2 * way, 2)], vol_relay.at[way])
        for way, step in ways
    ]
    vol_copies = [
        copy_to("z_hi", step, vol_ref.at[pl.ds((z_hi + step) % 4 * 4, 4)], ext.at[:, 1 + z_hi, 1:5])
        for way, step in ways
    ]
    start = pl.multiple_of(core * 512 + (z_lo % 4) * 128, 128)
    share = pl.ds(start, 128)
    for (way, step), copy in zip(ways, vol_on):
        copy.wait_recv()
        vol_copies.append(
            copy_to(
                "z_hi", step, vol_relay.at[way],
                ext.at[2 * way : 2 * way + 2, 1 + (z_hi + 4 - step) % 4, 1:5],
            )
        )
    hi_weights = group_to(
        "z_hi", OTHERS,
        lambda step: (dense_w_hbm.at[share], gathered.at[step - 1, share]),
        gathered.at[:, share],
    )
    for copy in local:
        copy.wait()
    for copy in vol_copies:
        copy.wait_recv()
    y_halo = [
        copy_to("y", 1, ext.at[:, 4, 1:5], ext.at[:, 0, 1:5]),
        copy_to("y", 3, ext.at[:, 1, 1:5], ext.at[:, 5, 1:5]),
    ]
    x_halo = [
        copy_to("x", 1, ext.at[:, 1:5, 4], ext.at[:, 1:5, 0]),
        copy_to("x", 3, ext.at[:, 1:5, 1], ext.at[:, 1:5, 5]),
    ]
    for kind, (dy, dx) in CORNERS:
        src = ext.at[:, 4 if dy == 1 else 1, 4 if dx == 1 else 1]
        dst = ext.at[:, 0 if dy == 1 else 5, 0 if dx == 1 else 5]
        x_halo.append(copy_to(kind, (dy, dx), src, dst))
    hi_weights.wait()
    lo_weights = group_to(
        "z_four", (1, 2, 3),
        lambda step: (gathered.at[:, share], gathered.at[:, share]),
        gathered.at[:, 0:384],
    )
    for copy in x_halo + y_halo:
        copy.wait()
    for copy in vol_on + vol_copies:
        copy.wait_send()

    @pl.when(y == 0)
    def _():
        ext[:, 0] = jnp.zeros((4, 6, 16, 128), BF16)

    @pl.when(y == 3)
    def _():
        ext[:, 5] = jnp.zeros((4, 6, 16, 128), BF16)

    @pl.when(x == 0)
    def _():
        ext[:, :, 0] = jnp.zeros((4, 6, 16, 128), BF16)

    @pl.when(x == 3)
    def _():
        ext[:, :, 5] = jnp.zeros((4, 6, 16, 128), BF16)

    def forward(s, carry):
        cells = ext[s].reshape(36, 16, 128).astype(F32)
        edge = jnp.zeros((36, 1, 128), F32)
        wide[s, :, :, :, 0:128] = (
            jnp.concatenate([edge, cells[:, :15]], axis=1).astype(BF16).reshape(6, 6, 16, 128)
        )
        wide[s, :, :, :, 128:256] = ext[s]
        wide[s, :, :, :, 256:384] = (
            jnp.concatenate([cells[:, 1:], edge], axis=1).astype(BF16).reshape(6, 6, 16, 128)
        )
        pre = jnp.zeros((256, 256), F32)
        for tap in range(9):
            a, b = tap // 3, tap % 3
            pre = pre + jnp.dot(
                wide[s, a : a + 4, b : b + 4].reshape(256, 384),
                weight_ref[tap * 384 : tap * 384 + 384],
                preferred_element_type=F32,
            )
        active, slope = gelu_and_slope(pre)
        slope_at[s] = slope
        summed[s] = jnp.sum(active.reshape(4, 4, 16, 256), axis=1).reshape(64, 256)
        return carry

    lax.fori_loop(0, 4, forward, 0)
    lo_weights.wait()
    half_rows = pl.ds(pl.multiple_of(core * 512, 512), 512)
    pair_weights = copy_to("core", 1, gathered.at[:, half_rows], gathered.at[:, half_rows])

    spread = one_hot(
        (256, 256),
        lambda r, c: (r // 64 == c // 16 % 4)
        & (r // 16 % 4 == c % 16 // 4)
        & (r % 16 == z_hi * 4 + c // 64),
        F32,
        1.0 / 16,
    )
    pooled = jnp.dot(
        spread, summed[...].reshape(256, 256), precision=EXACT, preferred_element_type=F32
    ).astype(BF16)
    pool[...] = pooled.reshape(4, 4, 16, 256)
    order = one_hot(
        (64, 256),
        lambda r, c: (r // 16 == c // 64)
        & (r // 4 % 4 == c // 16 % 4)
        & (z_hi * 4 + r % 4 == c % 16),
        BF16,
    )
    pool_out[...] = (
        jnp.dot(order, pooled, preferred_element_type=F32).astype(BF16).reshape(4, 16, 256)
    )
    pool_in[z_hi] = pool_out[z_hi]
    pool_copies = group_to(
        "z_hi", OTHERS,
        lambda step: (pool_out.at[(z_hi + step) % 4], pool_in.at[z_hi]),
        pool_in.at[0:3],
    )
    total = jnp.zeros((16, 128), F32)
    for k in range(4):
        if k == 1:
            pair_weights.wait()
        for block in range(4):
            rows = slice(block * 256, block * 256 + 256)
            total = total + jnp.dot(
                pool[(z_hi - k + 4) % 4, block],
                dense_w_ref[rows] if k == 0 else gathered[k - 1, rows],
                preferred_element_type=F32,
            )
    for stage, (kind, mine) in enumerate((("x", x), ("y", y))):
        held[stage, mine] = total
        group_to(
            kind, OTHERS,
            lambda step: (held.at[stage, mine], held.at[stage, mine]),
            held.at[stage, 0:3],
        ).wait()
        total = (held[stage, 0] + held[stage, 1]) + (held[stage, 2] + held[stage, 3])
    first = total
    out_w = jnp.concatenate([out_w_ref[...], jnp.zeros((124, 64), F32)], axis=0)
    across = (((1,), (1,)), ((), ()))
    targets = lax.dot_general(
        one_hot((16, 16), lambda r, c: r == c, F32),
        jnp.concatenate([targets_ref[...], jnp.zeros((124, 16), F32)], axis=0),
        across, precision=EXACT, preferred_element_type=F32,
    )
    first_gelu, first_slope = gelu_and_slope(first)
    second = lax.dot_general(
        first_gelu, mid_ref[...], across, precision=EXACT, preferred_element_type=F32
    )
    second_gelu, second_slope = gelu_and_slope(second)
    pred = lax.dot_general(second_gelu, out_w, across, precision=EXACT, preferred_element_type=F32)
    slope2 = second_slope * jnp.dot(
        pred - targets, out_w, precision=EXACT, preferred_element_type=F32
    )
    slope1 = first_slope * jnp.dot(
        slope2, mid_ref[...], precision=EXACT, preferred_element_type=F32
    )
    ours = lax.broadcasted_iota(jnp.int32, (16, 128), 0) // 4 == z_hi
    slope1 = jnp.where(ours, slope1, 0.0).astype(BF16)
    preds[z_hi] = jnp.where(ours, pred, 0.0)
    slope_in[z_hi] = slope1
    slope_copies = group_to(
        "z_hi", OTHERS, lambda step: (slope_in.at[z_hi], slope_in.at[z_hi]), slope_in.at[0:3]
    )
    pred_copies = group_to(
        "z_hi", OTHERS, lambda step: (preds.at[z_hi], preds.at[z_hi]), preds.at[0:3]
    )
    for k in range(4):
        for block in range(4):
            rows = slice(block * 256, block * 256 + 256)
            back[(z_hi - k + 4) % 4, block] = lax.dot_general(
                slope1, dense_w_ref[rows] if k == 0 else gathered[k - 1, rows], across,
                preferred_element_type=F32,
            )
    held_back = lax.dot_general(
        spread, back[...].reshape(256, 256), (((0,), (0,)), ((), ())), precision=EXACT,
        preferred_element_type=F32,
    )
    summed[...] = held_back.reshape(4, 64, 256)

    def turn(s, carry):
        spread_s = jnp.broadcast_to(summed[s].reshape(4, 1, 16, 256), (4, 4, 16, 256))
        cell = (spread_s.reshape(256, 256) * slope_at[s]).T.astype(BF16)
        for block in range(16):
            new = block % 2 * 8 + block // 2
            turned[s, new * 16 : new * 16 + 16] = cell[block * 16 : block * 16 + 16]
        return carry

    lax.fori_loop(0, 4, turn, 0)
    mine = pl.ds(pl.multiple_of(core * 128, 128), 128)
    theirs = pl.ds(pl.multiple_of(128 - core * 128, 128), 128)
    y_at = reserve(4)
    core_copies = []

    def y_copy(block, from_y):
        return pltpu.make_async_remote_copy(
            src_ref=y_out.at[block], dst_ref=y_in.at[from_y],
            send_sem=send_sem.at[y_at + block], recv_sem=recv_sem.at[y_at + from_y],
            device_id=partner("y", block - y + 4), device_id_type=MESH,
        )

    def over_y(block):
        core_copies[block].wait_recv()
        rows = slice(block * 864, block * 864 + 864)
        total = kern[rows, mine].astype(F32) + core_in[block].astype(F32)

        @pl.when(y == block)
        def _():
            y_sum[0:864] = total

        @pl.when(y != block)
        def _():
            y_out[block] = total.astype(BF16)
            y_copy(block, y).start()

    def hand_pooled():
        pool_copies.wait()
        order = one_hot(
            (64, 64),
            lambda r, c: (r // 16 == c // 4 % 4) & (r % 16 == c // 16 * 4 + c % 4),
            BF16,
        )
        rows = jnp.dot(order, pool_in[...].reshape(64, 256), preferred_element_type=F32)
        feat[core, z_lo] = rows.astype(BF16).reshape(4, 16, 256)
        return group_to(
            "z_lo", OCTET, lambda step: (feat.at[core, z_lo], feat.at[core, z_lo]), feat.at[core, 0:7]
        )

    def hand_slopes():
        slope_copies.wait()
        rows = (slope_in[0].astype(F32) + slope_in[1].astype(F32)) + (
            slope_in[2].astype(F32) + slope_in[3].astype(F32)
        )
        slopes[core, z_lo] = rows.astype(BF16)
        return group_to(
            "z_lo", OCTET,
            lambda step: (slopes.at[core, z_lo], slopes.at[core, z_lo]),
            slopes.at[core, 0:7],
        )

    for tap in range(9):
        a, b = tap // 3, tap % 3
        total = jnp.zeros((256, 384), F32)
        for s in range(4):
            total = total + jnp.dot(
                turned[s], wide[s, a : a + 4, b : b + 4].reshape(256, 384), preferred_element_type=F32
            )
        kern[tap * 384 : tap * 384 + 384] = total.T.astype(BF16)
        if tap in (2, 4, 6, 8):
            block = tap // 2 - 1
            rows = slice(block * 864, block * 864 + 864)
            core_copies.append(copy_to("core", 1, kern.at[rows, theirs], core_in.at[block]))
        if tap in (3, 5, 7):
            over_y(tap // 2 - 1)
        if tap == 5:
            feat_copies = hand_pooled()
    over_y(3)
    lo_slopes = hand_slopes()
    y_sum[864:896] = jnp.zeros((32, 128), F32)
    for block in range(4):

        @pl.when(y != block)
        def _(block=block):
            y_copy(block, block).wait()
            y_sum[0:864] = y_sum[0:864] + y_in[block].astype(F32)

    for hi in range(4):
        for to in range(4):
            start = (hi * 4 + to) * 54
            x_out[to, hi] = y_sum[start : start + 64].astype(BF16)
    group_to(
        "x", OTHERS, lambda step: (x_out.at[(x + step) % 4], x_in.at[step - 1]), x_in.at[0:3]
    ).wait()
    blocks = (x_out[x].astype(F32) + x_in[0].astype(F32)) + (x_in[1].astype(F32) + x_in[2].astype(F32))
    for half in range(2):
        both = jnp.concatenate([blocks[2 * half].T, blocks[2 * half + 1].T], axis=1)
        lo_out[:, half] = both.reshape(8, 16, 128).astype(BF16)
    turn_copies = group_to(
        "z_lo", OCTET, lambda step: (lo_out.at[(z_lo + step) % 8], lo_in.at[step - 1]), lo_in.at[0:7]
    )
    feat_copies.wait()
    lo_slopes.wait()
    pair = [
        copy_to("core", 1, feat.at[core], feat.at[core]),
        copy_to("core", 1, slopes.at[core], slopes.at[core]),
    ]
    turn_copies.wait()
    total = lo_out[z_lo].astype(F32)
    for step in range(7):
        total = total + lo_in[step].astype(F32)
    hi_out[...] = total
    hi_copies = group_to(
        "z_hi", OTHERS,
        lambda step: (hi_out.at[((z_hi + step) % 4) // 2], hi_in.at[step - 1]),
        hi_in.at[0:3],
    )
    for copy in pair:
        copy.wait()
    over = (((0,), (0,)), ((), ()))
    for block in range(4):
        sums = [
            lax.dot_general(
                feat[c, :, block].reshape(128, 256), slopes[c].reshape(128, 128), over,
                preferred_element_type=F32,
            )
            for c in range(2)
        ]
        dense_ref[block * 256 : block * 256 + 256] = sums[0] + sums[1]
    pred_copies.wait()
    sums = (preds[0] + preds[1]) + (preds[2] + preds[3])
    pred_ref[...] = jnp.concatenate([sums, jnp.zeros((112, 128), F32)], axis=0).T[0:4, 0:16]
    hi_copies.wait()
    total = (hi_out[z_hi // 2] + hi_in[0]) + (hi_in[1] + hi_in[2])
    conv_ref[...] = jnp.where(z_hi % 2 == 0, total[:, 0:54], total[:, 64:118])
    for copy in core_copies:
        copy.wait_send()
    assert used[0] == COPIES


def per_device(volume, conv_weight, dense_weight, mid_weight, out_weight, targets):
    vmem = pl.BlockSpec(memory_space=pltpu.VMEM)
    hbm = pl.BlockSpec(memory_space=pltpu.HBM)
    predictions, dense_grad, conv_grad = pl.pallas_call(
        kernel,
        name="conv_and_head",
        out_shape=(
            jax.ShapeDtypeStruct((4, 16), F32),
            jax.ShapeDtypeStruct((1024, 128), F32),
            jax.ShapeDtypeStruct((16, 54), F32),
        ),
        in_specs=[hbm] * 6,
        out_specs=(vmem,) * 3,
        scratch_shapes=[
            pltpu.VMEM((3456, 256), BF16),
            pltpu.VMEM((1024, 128), BF16),
            pltpu.VMEM((64, 128), F32),
            pltpu.VMEM((4, 64), F32),
            pltpu.VMEM((4, 16), F32),
            pltpu.VMEM((4, 6, 6, 16, 128), BF16),
            pltpu.VMEM((4, 6, 6, 16, 384), BF16),
            pltpu.VMEM((4, 256, 256), F32),
            pltpu.VMEM((4, 64, 256), F32),
            pltpu.VMEM((4, 4, 16, 256), BF16),
            pltpu.VMEM((4, 16, 256), BF16),
            pltpu.VMEM((4, 16, 256), BF16),
            pltpu.VMEM((2, 2, 4, 16, 128), BF16),
            pltpu.VMEM((3, 1024, 128), BF16),
            pltpu.VMEM((2, 4, 16, 128), F32),
            pltpu.VMEM((4, 4, 16, 256), F32),
            pltpu.VMEM((4, 256, 256), BF16),
            pltpu.VMEM((4, 16, 128), F32),
            pltpu.VMEM((3456, 256), BF16),
            pltpu.VMEM((4, 864, 128), BF16),
            pltpu.VMEM((4, 864, 128), BF16),
            pltpu.VMEM((4, 864, 128), BF16),
            pltpu.VMEM((896, 128), F32),
            pltpu.VMEM((4, 4, 64, 128), BF16),
            pltpu.VMEM((3, 4, 64, 128), BF16),
            pltpu.VMEM((8, 2, 16, 128), BF16),
            pltpu.VMEM((7, 2, 16, 128), BF16),
            pltpu.VMEM((2, 16, 128), F32),
            pltpu.VMEM((3, 16, 128), F32),
            pltpu.VMEM((2, 8, 4, 16, 256), BF16),
            pltpu.VMEM((2, 8, 16, 128), BF16),
            pltpu.VMEM((4, 16, 128), BF16),
            pltpu.SemaphoreType.DMA((COPIES,)),
            pltpu.SemaphoreType.DMA((COPIES,)),
            pltpu.SemaphoreType.DMA((6,)),
        ],
        compiler_params=pltpu.CompilerParams(
            collective_id=0, has_side_effects=True, vmem_limit_bytes=40 * 2**20
        ),
    )(
        *(
            pltpu.with_memory_space_constraint(array, pltpu.HBM)
            for array in (
                volume.reshape(16, 4, 16, 128),
                conv_weight,
                dense_weight.reshape(1024, 128),
                mid_weight.T,
                out_weight.T,
                targets.T,
            )
        )
    )
    return predictions.T, dense_grad.reshape(dense_weight.shape), conv_grad.T


def solution(mesh):
    in_specs = (
        P("sample", "depth", "height", None, None),
        P(),
        P("depth", "height", None, None),
        P(),
        P(),
        P("sample", None),
    )
    out_specs = (
        P("sample", None),
        P("depth", "height", None, None),
        P(("depth", "height"), "sample"),
    )
    return jax.shard_map(
        per_device, mesh=mesh, in_specs=in_specs, out_specs=out_specs, check_vma=False
    )
```

```python
import jax
import jax.numpy as jnp
from jax import lax
from jax.experimental import pallas as pl
from jax.experimental.pallas import tpu as pltpu
from jax.sharding import PartitionSpec as P

F32 = jnp.float32
BF16 = jnp.bfloat16
MESH = pl.DeviceIdType.MESH
EXACT = lax.Precision.HIGHEST


def place():
    sample, depth, x = lax.axis_index("sample"), lax.axis_index("depth"), lax.axis_index("height")
    return sample // 2, sample % 2, depth // 4, depth % 4, x


def partner(kind, step):
    z_lo, core, y, z_hi, x = place()
    if kind == "z_lo":
        z_lo = (z_lo + step) % 8
    elif kind == "z_four":
        z_lo = (z_lo // 4) * 4 + (z_lo + step) % 4
    elif kind == "core":
        core = (core + step) % 2
    elif kind == "y":
        y = (y + step) % 4
    elif kind == "z_hi":
        z_hi = (z_hi + step) % 4
    elif kind == "x":
        x = (x + step) % 4
    else:
        y, x = (y + step[0]) % 4, (x + step[1]) % 4
    return (z_lo * 2 + core, y * 4 + z_hi, x)


QUADS = [(kind, step) for kind in ("x", "y", "z_hi") for step in (1, 2, 3)]
OTHERS = (2, 1, 3)
OCTET = range(1, 8)
CORNERS = [("corner", (dy, dx)) for dy in (1, 3) for dx in (1, 3)]
PARTNERS = [("core", 1)] + [q for q in QUADS if q != ("z_hi", 2)] + [("z_lo", step) for step in OCTET] + CORNERS
COPIES = 42


def gelu_and_slope(value):
    rate = 0.7978845608028654
    square = value * value
    bend = jnp.tanh(rate * (value + 0.044715 * value * square))
    half = 0.5 * (1.0 + bend)
    slope = half + 0.5 * value * (1.0 - bend * bend) * (rate * (1.0 + 3 * 0.044715 * square))
    return value * half, slope


def one_hot(shape, test, kind, weight=1.0):
    row = lax.broadcasted_iota(jnp.int32, shape, 0)
    column = lax.broadcasted_iota(jnp.int32, shape, 1)
    return jnp.where(test(row, column), weight, 0.0).astype(kind)


def kernel(
    vol_ref, weight_hbm, dense_w_hbm, mid_hbm, out_w_hbm, targets_hbm,
    pred_ref, dense_ref, conv_ref,
    weight_ref, dense_w_ref, mid_ref, out_w_ref, targets_ref,
    ext, wide, slope_at, summed, pool, pool_out, pool_in, vol_relay, gathered, held, back, turned, preds,
    kern, core_in, y_out, y_in, y_sum, x_out, x_in,
    lower, x_first, x_first_in, y_last, y_last_in, lo_out, lo_in, hi_out, hi_in,
    feat, slopes, slope_in,
    send_sem, recv_sem, local_sem,
):
    z_lo, core, y, z_hi, x = place()
    used = [0]

    def reserve(count):
        used[0] += count
        assert used[0] <= COPIES
        return used[0] - count

    def copy_to(kind, step, src, dst):
        at = reserve(1)
        copy = pltpu.make_async_remote_copy(
            src_ref=src, dst_ref=dst, send_sem=send_sem.at[at], recv_sem=recv_sem.at[at],
            device_id=partner(kind, step), device_id_type=MESH,
        )
        copy.start()
        return copy

    def group_to(kind, steps, pair_of, span):
        at = reserve(1)
        sems = dict(send_sem=send_sem.at[at], recv_sem=recv_sem.at[at], device_id_type=MESH)
        for step in steps:
            src, dst = pair_of(step)
            pltpu.make_async_remote_copy(
                src_ref=src, dst_ref=dst, device_id=partner(kind, step), **sems
            ).start()
        return pltpu.make_async_remote_copy(
            src_ref=span, dst_ref=span, device_id=partner(kind, steps[0]), **sems
        )

    barrier = pltpu.get_barrier_semaphore()
    for kind, step in PARTNERS:
        pl.semaphore_signal(barrier, inc=1, device_id=partner(kind, step), device_id_type=MESH)
    local = [
        (vol_ref.at[pl.ds(z_hi * 4, 4)], ext.at[:, 1 + z_hi, 1:5]),
        (dense_w_hbm, dense_w_ref),
        (weight_hbm, weight_ref),
        (mid_hbm, mid_ref),
        (out_w_hbm, out_w_ref),
        (targets_hbm, targets_ref),
    ]
    local = [pltpu.make_async_copy(src, dst, local_sem.at[at]) for at, (src, dst) in enumerate(local)]
    for copy in local:
        copy.start()
    pl.semaphore_wait(barrier, len(PARTNERS))

    far = (z_hi + 2) % 4
    ways = ((0, 1), (1, 3))
    vol_on = [
        copy_to("z_hi", step, vol_ref.at[pl.ds(far * 4 + 2 * way, 2)], vol_relay.at[way])
        for way, step in ways
    ]
    vol_copies = [
        copy_to("z_hi", step, vol_ref.at[pl.ds((z_hi + step) % 4 * 4, 4)], ext.at[:, 1 + z_hi, 1:5])
        for way, step in ways
    ]
    start = pl.multiple_of(core * 512 + (z_lo % 4) * 128, 128)
    share = pl.ds(start, 128)
    for (way, step), copy in zip(ways, vol_on):
        copy.wait_recv()
        vol_copies.append(
            copy_to(
                "z_hi", step, vol_relay.at[way],
                ext.at[2 * way : 2 * way + 2, 1 + (z_hi + 4 - step) % 4, 1:5],
            )
        )
    hi_weights = group_to(
        "z_hi", OTHERS,
        lambda step: (dense_w_hbm.at[share], gathered.at[step - 1, share]),
        gathered.at[:, share],
    )
    for copy in local:
        copy.wait()
    for copy in vol_copies:
        copy.wait_recv()
    y_halo = [
        copy_to("y", 1, ext.at[:, 4, 1:5], ext.at[:, 0, 1:5]),
        copy_to("y", 3, ext.at[:, 1, 1:5], ext.at[:, 5, 1:5]),
    ]
    x_halo = [
        copy_to("x", 1, ext.at[:, 1:5, 4], ext.at[:, 1:5, 0]),
        copy_to("x", 3, ext.at[:, 1:5, 1], ext.at[:, 1:5, 5]),
    ]
    for kind, (dy, dx) in CORNERS:
        src = ext.at[:, 4 if dy == 1 else 1, 4 if dx == 1 else 1]
        dst = ext.at[:, 0 if dy == 1 else 5, 0 if dx == 1 else 5]
        x_halo.append(copy_to(kind, (dy, dx), src, dst))
    hi_weights.wait()
    lo_weights = group_to(
        "z_four", (1, 2, 3),
        lambda step: (gathered.at[:, share], gathered.at[:, share]),
        gathered.at[:, 0:384],
    )
    for copy in x_halo + y_halo:
        copy.wait()
    for copy in vol_on + vol_copies:
        copy.wait_send()

    @pl.when(y == 0)
    def _():
        ext[:, 0] = jnp.zeros((4, 6, 16, 128), BF16)

    @pl.when(y == 3)
    def _():
        ext[:, 5] = jnp.zeros((4, 6, 16, 128), BF16)

    @pl.when(x == 0)
    def _():
        ext[:, :, 0] = jnp.zeros((4, 6, 16, 128), BF16)

    @pl.when(x == 3)
    def _():
        ext[:, :, 5] = jnp.zeros((4, 6, 16, 128), BF16)

    def forward(s, carry):
        cells = ext[s].reshape(36, 16, 128).astype(F32)
        edge = jnp.zeros((36, 1, 128), F32)
        wide[s, :, :, :, 0:128] = (
            jnp.concatenate([edge, cells[:, :15]], axis=1).astype(BF16).reshape(6, 6, 16, 128)
        )
        wide[s, :, :, :, 128:256] = ext[s]
        wide[s, :, :, :, 256:384] = (
            jnp.concatenate([cells[:, 1:], edge], axis=1).astype(BF16).reshape(6, 6, 16, 128)
        )
        pre = jnp.zeros((256, 256), F32)
        for tap in range(9):
            a, b = tap // 3, tap % 3
            pre = pre + jnp.dot(
                wide[s, a : a + 4, b : b + 4].reshape(256, 384),
                weight_ref[tap * 384 : tap * 384 + 384],
                preferred_element_type=F32,
            )
        active, slope = gelu_and_slope(pre)
        slope_at[s] = slope
        summed[s] = jnp.sum(active.reshape(4, 4, 16, 256), axis=1).reshape(64, 256)
        return carry

    lax.fori_loop(0, 4, forward, 0)
    lo_weights.wait()
    half_rows = pl.ds(pl.multiple_of(core * 512, 512), 512)
    pair_weights = copy_to("core", 1, gathered.at[:, half_rows], gathered.at[:, half_rows])

    spread = one_hot(
        (256, 256),
        lambda r, c: (r // 64 == c // 16 % 4)
        & (r // 16 % 4 == c % 16 // 4)
        & (r % 16 == z_hi * 4 + c // 64),
        F32,
        1.0 / 16,
    )
    pooled = jnp.dot(
        spread, summed[...].reshape(256, 256), precision=EXACT, preferred_element_type=F32
    ).astype(BF16)
    pool[...] = pooled.reshape(4, 4, 16, 256)
    order = one_hot(
        (64, 256),
        lambda r, c: (r // 16 == c // 64)
        & (r // 4 % 4 == c // 16 % 4)
        & (z_hi * 4 + r % 4 == c % 16),
        BF16,
    )
    pool_out[...] = (
        jnp.dot(order, pooled, preferred_element_type=F32).astype(BF16).reshape(4, 16, 256)
    )
    pool_in[z_hi] = pool_out[z_hi]
    pool_copies = group_to(
        "z_hi", OTHERS,
        lambda step: (pool_out.at[(z_hi + step) % 4], pool_in.at[z_hi]),
        pool_in.at[0:3],
    )
    total = jnp.zeros((16, 128), F32)
    for k in range(4):
        if k == 1:
            pair_weights.wait()
        for block in range(4):
            rows = slice(block * 256, block * 256 + 256)
            total = total + jnp.dot(
                pool[(z_hi - k + 4) % 4, block],
                dense_w_ref[rows] if k == 0 else gathered[k - 1, rows],
                preferred_element_type=F32,
            )
    for stage, (kind, mine) in enumerate((("x", x), ("y", y))):
        held[stage, mine] = total
        group_to(
            kind, OTHERS,
            lambda step: (held.at[stage, mine], held.at[stage, mine]),
            held.at[stage, 0:3],
        ).wait()
        total = (held[stage, 0] + held[stage, 1]) + (held[stage, 2] + held[stage, 3])
    first = total
    out_w = jnp.concatenate([out_w_ref[...], jnp.zeros((124, 64), F32)], axis=0)
    across = (((1,), (1,)), ((), ()))
    targets = lax.dot_general(
        one_hot((16, 16), lambda r, c: r == c, F32),
        jnp.concatenate([targets_ref[...], jnp.zeros((124, 16), F32)], axis=0),
        across, precision=EXACT, preferred_element_type=F32,
    )
    first_gelu, first_slope = gelu_and_slope(first)
    second = lax.dot_general(
        first_gelu, mid_ref[...], across, precision=EXACT, preferred_element_type=F32
    )
    second_gelu, second_slope = gelu_and_slope(second)
    pred = lax.dot_general(second_gelu, out_w, across, precision=EXACT, preferred_element_type=F32)
    slope2 = second_slope * jnp.dot(
        pred - targets, out_w, precision=EXACT, preferred_element_type=F32
    )
    slope1 = first_slope * jnp.dot(
        slope2, mid_ref[...], precision=EXACT, preferred_element_type=F32
    )
    ours = lax.broadcasted_iota(jnp.int32, (16, 128), 0) // 4 == z_hi
    slope1 = jnp.where(ours, slope1, 0.0).astype(BF16)
    preds[z_hi] = jnp.where(ours, pred, 0.0)
    slope_in[z_hi] = slope1
    slope_copies = group_to(
        "z_hi", OTHERS, lambda step: (slope_in.at[z_hi], slope_in.at[z_hi]), slope_in.at[0:3]
    )
    pred_copies = group_to(
        "z_hi", OTHERS, lambda step: (preds.at[z_hi], preds.at[z_hi]), preds.at[0:3]
    )
    for k in range(4):
        for block in range(4):
            rows = slice(block * 256, block * 256 + 256)
            back[(z_hi - k + 4) % 4, block] = lax.dot_general(
                slope1, dense_w_ref[rows] if k == 0 else gathered[k - 1, rows], across,
                preferred_element_type=F32,
            )
    held_back = lax.dot_general(
        spread, back[...].reshape(256, 256), (((0,), (0,)), ((), ())), precision=EXACT,
        preferred_element_type=F32,
    )
    summed[...] = held_back.reshape(4, 64, 256)

    def turn(s, carry):
        spread_s = jnp.broadcast_to(summed[s].reshape(4, 1, 16, 256), (4, 4, 16, 256))
        cell = (spread_s.reshape(256, 256) * slope_at[s]).T.astype(BF16)
        for block in range(16):
            new = block % 2 * 8 + block // 2
            turned[s, new * 16 : new * 16 + 16] = cell[block * 16 : block * 16 + 16]
        return carry

    lax.fori_loop(0, 4, turn, 0)
    mine = pl.ds(pl.multiple_of(core * 128, 128), 128)
    theirs = pl.ds(pl.multiple_of(128 - core * 128, 128), 128)
    y_at = reserve(4)
    core_copies, x_first_copies = [], []
    lower[432:448] = jnp.zeros((16, 128), F32)

    def y_copy(block, from_y):
        return pltpu.make_async_remote_copy(
            src_ref=y_out.at[block], dst_ref=y_in.at[from_y],
            send_sem=send_sem.at[y_at + block], recv_sem=recv_sem.at[y_at + from_y],
            device_id=partner("y", block - y + 4), device_id_type=MESH,
        )

    def over_y(block):
        core_copies[block].wait_recv()
        rows = slice(block * 864, block * 864 + 864)
        total = kern[rows, mine].astype(F32) + core_in[block].astype(F32)

        @pl.when(y == block)
        def _():
            y_sum[0:432] = total[0:432]

        @pl.when(y != block)
        def _():
            y_out[block] = total[0:432].astype(BF16)
            y_copy(block, y).start()

        lower[0:432] = total[432:864]
        for hi in range(2):
            for to in range(4):
                start = (hi * 4 + to) * 54
                x_first[to, block, hi] = lower[start : start + 64].astype(BF16)
        x_first_copies.append(
            group_to(
                "x", OTHERS,
                lambda step: (x_first.at[(x + step) % 4, block], x_first_in.at[block, step - 1]),
                x_first_in.at[block],
            )
        )

    def hand_pooled():
        pool_copies.wait()
        order = one_hot(
            (64, 64),
            lambda r, c: (r // 16 == c // 4 % 4) & (r % 16 == c // 16 * 4 + c % 4),
            BF16,
        )
        rows = jnp.dot(order, pool_in[...].reshape(64, 256), preferred_element_type=F32)
        feat[core, z_lo] = rows.astype(BF16).reshape(4, 16, 256)
        return group_to(
            "z_lo", OCTET, lambda step: (feat.at[core, z_lo], feat.at[core, z_lo]), feat.at[core, 0:7]
        )

    def hand_slopes():
        slope_copies.wait()
        rows = (slope_in[0].astype(F32) + slope_in[1].astype(F32)) + (
            slope_in[2].astype(F32) + slope_in[3].astype(F32)
        )
        slopes[core, z_lo] = rows.astype(BF16)
        return group_to(
            "z_lo", OCTET,
            lambda step: (slopes.at[core, z_lo], slopes.at[core, z_lo]),
            slopes.at[core, 0:7],
        )

    for tap in range(9):
        a, b = tap // 3, tap % 3
        total = jnp.zeros((256, 384), F32)
        for s in range(4):
            total = total + jnp.dot(
                turned[s], wide[s, a : a + 4, b : b + 4].reshape(256, 384), preferred_element_type=F32
            )
        kern[tap * 384 : tap * 384 + 384] = total.T.astype(BF16)
        if tap in (2, 4, 6, 8):
            block = tap // 2 - 1
            rows = slice(block * 864, block * 864 + 864)
            core_copies.append(copy_to("core", 1, kern.at[rows, theirs], core_in.at[block]))
        if tap in (3, 5, 7):
            over_y(tap // 2 - 1)
        if tap == 5:
            feat_copies = hand_pooled()
    over_y(3)
    lo_slopes = hand_slopes()
    y_sum[432:448] = jnp.zeros((16, 128), F32)
    for block in range(4):

        @pl.when(y != block)
        def _(block=block):
            y_copy(block, block).wait()
            y_sum[0:432] = y_sum[0:432] + y_in[block].astype(F32)

    for hi in range(2):
        for to in range(4):
            start = (hi * 4 + to) * 54
            x_out[to, hi] = y_sum[start : start + 64].astype(BF16)
    x_copies = group_to(
        "x", OTHERS, lambda step: (x_out.at[(x + step) % 4], x_in.at[step - 1]), x_in.at[0:3]
    )
    for block in range(4):
        x_first_copies[block].wait()
        y_last[block] = (
            (x_first[x, block].astype(F32) + x_first_in[block, 0].astype(F32))
            + (x_first_in[block, 1].astype(F32) + x_first_in[block, 2].astype(F32))
        ).astype(BF16)
    y_last_copies = group_to(
        "y", OTHERS,
        lambda step: (y_last.at[(y + step) % 4], y_last_in.at[step - 1]),
        y_last_in.at[0:3],
    )
    x_copies.wait()
    upper_blocks = (x_out[x].astype(F32) + x_in[0].astype(F32)) + (
        x_in[1].astype(F32) + x_in[2].astype(F32)
    )
    y_last_copies.wait()
    lower_blocks = (y_last[y].astype(F32) + y_last_in[0].astype(F32)) + (
        y_last_in[1].astype(F32) + y_last_in[2].astype(F32)
    )
    for half, blocks in enumerate((upper_blocks, lower_blocks)):
        both = jnp.concatenate([blocks[0].T, blocks[1].T], axis=1)
        lo_out[:, half] = both.reshape(8, 16, 128).astype(BF16)
    turn_copies = group_to(
        "z_lo", OCTET, lambda step: (lo_out.at[(z_lo + step) % 8], lo_in.at[step - 1]), lo_in.at[0:7]
    )
    feat_copies.wait()
    lo_slopes.wait()
    pair = [
        copy_to("core", 1, feat.at[core], feat.at[core]),
        copy_to("core", 1, slopes.at[core], slopes.at[core]),
    ]
    turn_copies.wait()
    total = lo_out[z_lo].astype(F32)
    for step in range(7):
        total = total + lo_in[step].astype(F32)
    for hi in range(4):
        lanes = slice(hi % 2 * 64, hi % 2 * 64 + 64)
        hi_out[hi] = jnp.concatenate([total[hi // 2, 0:8, lanes], total[hi // 2, 8:16, lanes]], axis=1)
    hi_copies = group_to(
        "z_hi", OTHERS,
        lambda step: (hi_out.at[(z_hi + step) % 4], hi_in.at[step - 1]),
        hi_in.at[0:3],
    )
    for copy in pair:
        copy.wait()
    over = (((0,), (0,)), ((), ()))
    for block in range(4):
        sums = [
            lax.dot_general(
                feat[c, :, block].reshape(128, 256), slopes[c].reshape(128, 128), over,
                preferred_element_type=F32,
            )
            for c in range(2)
        ]
        dense_ref[block * 256 : block * 256 + 256] = sums[0] + sums[1]
    pred_copies.wait()
    sums = (preds[0] + preds[1]) + (preds[2] + preds[3])
    pred_ref[...] = jnp.concatenate([sums, jnp.zeros((112, 128), F32)], axis=0).T[0:4, 0:16]
    hi_copies.wait()
    total = (hi_out[z_hi] + hi_in[0]) + (hi_in[1] + hi_in[2])
    conv_ref[0:8] = total[:, 0:54]
    conv_ref[8:16] = total[:, 64:118]
    for copy in core_copies:
        copy.wait_send()
    assert used[0] == COPIES


def per_device(volume, conv_weight, dense_weight, mid_weight, out_weight, targets):
    vmem = pl.BlockSpec(memory_space=pltpu.VMEM)
    hbm = pl.BlockSpec(memory_space=pltpu.HBM)
    predictions, dense_grad, conv_grad = pl.pallas_call(
        kernel,
        name="conv_and_head",
        out_shape=(
            jax.ShapeDtypeStruct((4, 16), F32),
            jax.ShapeDtypeStruct((1024, 128), F32),
            jax.ShapeDtypeStruct((16, 54), F32),
        ),
        in_specs=[hbm] * 6,
        out_specs=(vmem,) * 3,
        scratch_shapes=[
            pltpu.VMEM((3456, 256), BF16),
            pltpu.VMEM((1024, 128), BF16),
            pltpu.VMEM((64, 128), F32),
            pltpu.VMEM((4, 64), F32),
            pltpu.VMEM((4, 16), F32),
            pltpu.VMEM((4, 6, 6, 16, 128), BF16),
            pltpu.VMEM((4, 6, 6, 16, 384), BF16),
            pltpu.VMEM((4, 256, 256), F32),
            pltpu.VMEM((4, 64, 256), F32),
            pltpu.VMEM((4, 4, 16, 256), BF16),
            pltpu.VMEM((4, 16, 256), BF16),
            pltpu.VMEM((4, 16, 256), BF16),
            pltpu.VMEM((2, 2, 4, 16, 128), BF16),
            pltpu.VMEM((3, 1024, 128), BF16),
            pltpu.VMEM((2, 4, 16, 128), F32),
            pltpu.VMEM((4, 4, 16, 256), F32),
            pltpu.VMEM((4, 256, 256), BF16),
            pltpu.VMEM((4, 16, 128), F32),
            pltpu.VMEM((3456, 256), BF16),
            pltpu.VMEM((4, 864, 128), BF16),
            pltpu.VMEM((4, 432, 128), BF16),
            pltpu.VMEM((4, 432, 128), BF16),
            pltpu.VMEM((448, 128), F32),
            pltpu.VMEM((4, 2, 64, 128), BF16),
            pltpu.VMEM((3, 2, 64, 128), BF16),
            pltpu.VMEM((448, 128), F32),
            pltpu.VMEM((4, 4, 2, 64, 128), BF16),
            pltpu.VMEM((4, 3, 2, 64, 128), BF16),
            pltpu.VMEM((4, 2, 64, 128), BF16),
            pltpu.VMEM((3, 2, 64, 128), BF16),
            pltpu.VMEM((8, 2, 16, 128), BF16),
            pltpu.VMEM((7, 2, 16, 128), BF16),
            pltpu.VMEM((4, 8, 128), F32),
            pltpu.VMEM((3, 8, 128), F32),
            pltpu.VMEM((2, 8, 4, 16, 256), BF16),
            pltpu.VMEM((2, 8, 16, 128), BF16),
            pltpu.VMEM((4, 16, 128), BF16),
            pltpu.SemaphoreType.DMA((COPIES,)),
            pltpu.SemaphoreType.DMA((COPIES,)),
            pltpu.SemaphoreType.DMA((6,)),
        ],
        compiler_params=pltpu.CompilerParams(
            collective_id=0, has_side_effects=True, vmem_limit_bytes=40 * 2**20
        ),
    )(
        *(
            pltpu.with_memory_space_constraint(array, pltpu.HBM)
            for array in (
                volume.reshape(16, 4, 16, 128),
                conv_weight,
                dense_weight.reshape(1024, 128),
                mid_weight.T,
                out_weight.T,
                targets.T,
            )
        )
    )
    return predictions.T, dense_grad.reshape(dense_weight.shape), conv_grad.T


def solution(mesh):
    in_specs = (
        P("sample", "depth", "height", None, None),
        P(),
        P("depth", "height", None, None),
        P(),
        P(),
        P("sample", None),
    )
    out_specs = (
        P("sample", None),
        P("depth", "height", None, None),
        P(("depth", "height"), "sample"),
    )
    return jax.shard_map(
        per_device, mesh=mesh, in_specs=in_specs, out_specs=out_specs, check_vma=False
    )
```

```python
import jax
import jax.numpy as jnp
from jax import lax
from jax.experimental import pallas as pl
from jax.experimental.pallas import tpu as pltpu
from jax.sharding import PartitionSpec as P

F32 = jnp.float32
BF16 = jnp.bfloat16
MESH = pl.DeviceIdType.MESH
EXACT = lax.Precision.HIGHEST


def place():
    sample, depth, x = lax.axis_index("sample"), lax.axis_index("depth"), lax.axis_index("height")
    return sample // 2, sample % 2, depth // 4, depth % 4, x


def partner(kind, step):
    z_lo, core, y, z_hi, x = place()
    if kind == "z_lo":
        z_lo = (z_lo + step) % 8
    elif kind == "z_four":
        z_lo = (z_lo // 4) * 4 + (z_lo + step) % 4
    elif kind == "core":
        core = (core + step) % 2
    elif kind == "y":
        y = (y + step) % 4
    elif kind == "z_hi":
        z_hi = (z_hi + step) % 4
    elif kind == "x":
        x = (x + step) % 4
    else:
        y, x = (y + step[0]) % 4, (x + step[1]) % 4
    return (z_lo * 2 + core, y * 4 + z_hi, x)


AROUND = [(dy, dx) for dy in (2, 1, 3, 0) for dx in (2, 1, 3, 0) if (dy, dx) != (0, 0)]
OTHERS = (2, 1, 3)
OCTET = range(1, 8)
CORNERS = [("corner", (dy, dx)) for dy in (1, 3) for dx in (1, 3)]
PARTNERS = [("core", 1)] + [("z_hi", 1), ("z_hi", 3)] + [("z_lo", step) for step in OCTET] + [("corner", step) for step in AROUND]
COPIES = 41


def gelu_and_slope(value):
    rate = 0.7978845608028654
    square = value * value
    bend = jnp.tanh(rate * (value + 0.044715 * value * square))
    half = 0.5 * (1.0 + bend)
    slope = half + 0.5 * value * (1.0 - bend * bend) * (rate * (1.0 + 3 * 0.044715 * square))
    return value * half, slope


def one_hot(shape, test, kind, weight=1.0):
    row = lax.broadcasted_iota(jnp.int32, shape, 0)
    column = lax.broadcasted_iota(jnp.int32, shape, 1)
    return jnp.where(test(row, column), weight, 0.0).astype(kind)


def kernel(
    vol_ref, weight_hbm, dense_w_hbm, mid_hbm, out_w_hbm, targets_hbm,
    pred_ref, dense_ref, conv_ref,
    weight_ref, dense_w_ref, mid_ref, out_w_ref, targets_ref,
    ext, wide, slope_at, summed, pool, pool_out, pool_in, vol_relay, gathered, held, back, turned, preds,
    kern, core_in, y_out, y_in, y_sum, x_out, x_in,
    lower, x_first, x_first_in, y_last, y_last_in, lo_out, lo_in, hi_out, hi_in,
    feat, slopes, slope_in,
    send_sem, recv_sem, local_sem,
):
    z_lo, core, y, z_hi, x = place()
    used = [0]

    def reserve(count):
        used[0] += count
        assert used[0] <= COPIES
        return used[0] - count

    def copy_to(kind, step, src, dst):
        at = reserve(1)
        copy = pltpu.make_async_remote_copy(
            src_ref=src, dst_ref=dst, send_sem=send_sem.at[at], recv_sem=recv_sem.at[at],
            device_id=partner(kind, step), device_id_type=MESH,
        )
        copy.start()
        return copy

    def group_to(kind, steps, pair_of, span):
        at = reserve(1)
        sems = dict(send_sem=send_sem.at[at], recv_sem=recv_sem.at[at], device_id_type=MESH)
        for step in steps:
            src, dst = pair_of(step)
            pltpu.make_async_remote_copy(
                src_ref=src, dst_ref=dst, device_id=partner(kind, step), **sems
            ).start()
        return pltpu.make_async_remote_copy(
            src_ref=span, dst_ref=span, device_id=partner(kind, steps[0]), **sems
        )

    barrier = pltpu.get_barrier_semaphore()
    for kind, step in PARTNERS:
        pl.semaphore_signal(barrier, inc=1, device_id=partner(kind, step), device_id_type=MESH)
    local = [
        (vol_ref.at[pl.ds(z_hi * 4, 4)], ext.at[:, 1 + z_hi, 1:5]),
        (dense_w_hbm, dense_w_ref),
        (weight_hbm, weight_ref),
        (mid_hbm, mid_ref),
        (out_w_hbm, out_w_ref),
        (targets_hbm, targets_ref),
    ]
    local = [pltpu.make_async_copy(src, dst, local_sem.at[at]) for at, (src, dst) in enumerate(local)]
    for copy in local:
        copy.start()
    pl.semaphore_wait(barrier, len(PARTNERS))

    far = (z_hi + 2) % 4
    ways = ((0, 1), (1, 3))
    vol_on = [
        copy_to("z_hi", step, vol_ref.at[pl.ds(far * 4 + 2 * way, 2)], vol_relay.at[way])
        for way, step in ways
    ]
    vol_copies = [
        copy_to("z_hi", step, vol_ref.at[pl.ds((z_hi + step) % 4 * 4, 4)], ext.at[:, 1 + z_hi, 1:5])
        for way, step in ways
    ]
    start = pl.multiple_of(core * 512 + (z_lo % 4) * 128, 128)
    share = pl.ds(start, 128)
    for (way, step), copy in zip(ways, vol_on):
        copy.wait_recv()
        vol_copies.append(
            copy_to(
                "z_hi", step, vol_relay.at[way],
                ext.at[2 * way : 2 * way + 2, 1 + (z_hi + 4 - step) % 4, 1:5],
            )
        )
    hi_weights = group_to(
        "z_hi", OTHERS,
        lambda step: (dense_w_hbm.at[share], gathered.at[step - 1, share]),
        gathered.at[:, share],
    )
    for copy in local:
        copy.wait()
    for copy in vol_copies:
        copy.wait_recv()
    y_halo = [
        copy_to("y", 1, ext.at[:, 4, 1:5], ext.at[:, 0, 1:5]),
        copy_to("y", 3, ext.at[:, 1, 1:5], ext.at[:, 5, 1:5]),
    ]
    x_halo = [
        copy_to("x", 1, ext.at[:, 1:5, 4], ext.at[:, 1:5, 0]),
        copy_to("x", 3, ext.at[:, 1:5, 1], ext.at[:, 1:5, 5]),
    ]
    for kind, (dy, dx) in CORNERS:
        src = ext.at[:, 4 if dy == 1 else 1, 4 if dx == 1 else 1]
        dst = ext.at[:, 0 if dy == 1 else 5, 0 if dx == 1 else 5]
        x_halo.append(copy_to(kind, (dy, dx), src, dst))
    hi_weights.wait()
    lo_weights = group_to(
        "z_four", (1, 2, 3),
        lambda step: (gathered.at[:, share], gathered.at[:, share]),
        gathered.at[:, 0:384],
    )
    for copy in x_halo + y_halo:
        copy.wait()
    for copy in vol_on + vol_copies:
        copy.wait_send()

    @pl.when(y == 0)
    def _():
        ext[:, 0] = jnp.zeros((4, 6, 16, 128), BF16)

    @pl.when(y == 3)
    def _():
        ext[:, 5] = jnp.zeros((4, 6, 16, 128), BF16)

    @pl.when(x == 0)
    def _():
        ext[:, :, 0] = jnp.zeros((4, 6, 16, 128), BF16)

    @pl.when(x == 3)
    def _():
        ext[:, :, 5] = jnp.zeros((4, 6, 16, 128), BF16)

    def forward(s, carry):
        cells = ext[s].reshape(36, 16, 128).astype(F32)
        edge = jnp.zeros((36, 1, 128), F32)
        wide[s, :, :, :, 0:128] = (
            jnp.concatenate([edge, cells[:, :15]], axis=1).astype(BF16).reshape(6, 6, 16, 128)
        )
        wide[s, :, :, :, 128:256] = ext[s]
        wide[s, :, :, :, 256:384] = (
            jnp.concatenate([cells[:, 1:], edge], axis=1).astype(BF16).reshape(6, 6, 16, 128)
        )
        pre = jnp.zeros((256, 256), F32)
        for tap in range(9):
            a, b = tap // 3, tap % 3
            pre = pre + jnp.dot(
                wide[s, a : a + 4, b : b + 4].reshape(256, 384),
                weight_ref[tap * 384 : tap * 384 + 384],
                preferred_element_type=F32,
            )
        active, slope = gelu_and_slope(pre)
        slope_at[s] = slope
        summed[s] = jnp.sum(active.reshape(4, 4, 16, 256), axis=1).reshape(64, 256)
        return carry

    lax.fori_loop(0, 4, forward, 0)
    lo_weights.wait()
    half_rows = pl.ds(pl.multiple_of(core * 512, 512), 512)
    pair_weights = copy_to("core", 1, gathered.at[:, half_rows], gathered.at[:, half_rows])

    spread = one_hot(
        (256, 256),
        lambda r, c: (r // 64 == c // 16 % 4)
        & (r // 16 % 4 == c % 16 // 4)
        & (r % 16 == z_hi * 4 + c // 64),
        F32,
        1.0 / 16,
    )
    pooled = jnp.dot(
        spread, summed[...].reshape(256, 256), precision=EXACT, preferred_element_type=F32
    ).astype(BF16)
    pool[...] = pooled.reshape(4, 4, 16, 256)
    order = one_hot(
        (64, 256),
        lambda r, c: (r // 16 == c // 64)
        & (r // 4 % 4 == c // 16 % 4)
        & (z_hi * 4 + r % 4 == c % 16),
        BF16,
    )
    pool_out[...] = (
        jnp.dot(order, pooled, preferred_element_type=F32).astype(BF16).reshape(4, 16, 256)
    )
    pool_in[z_hi] = pool_out[z_hi]
    pool_copies = group_to(
        "z_hi", OTHERS,
        lambda step: (pool_out.at[(z_hi + step) % 4], pool_in.at[z_hi]),
        pool_in.at[0:3],
    )
    total = jnp.zeros((16, 128), F32)
    for k in range(4):
        if k == 1:
            pair_weights.wait()
        for block in range(4):
            rows = slice(block * 256, block * 256 + 256)
            total = total + jnp.dot(
                pool[(z_hi - k + 4) % 4, block],
                dense_w_ref[rows] if k == 0 else gathered[k - 1, rows],
                preferred_element_type=F32,
            )
    here = y * 4 + x
    held[here] = total
    group_to("corner", AROUND, lambda step: (held.at[here], held.at[here]), held.at[0:15]).wait()
    total = held[0]
    for at in range(1, 16):
        total = total + held[at]
    first = total
    out_w = jnp.concatenate([out_w_ref[...], jnp.zeros((124, 64), F32)], axis=0)
    across = (((1,), (1,)), ((), ()))
    targets = lax.dot_general(
        one_hot((16, 16), lambda r, c: r == c, F32),
        jnp.concatenate([targets_ref[...], jnp.zeros((124, 16), F32)], axis=0),
        across, precision=EXACT, preferred_element_type=F32,
    )
    first_gelu, first_slope = gelu_and_slope(first)
    second = lax.dot_general(
        first_gelu, mid_ref[...], across, precision=EXACT, preferred_element_type=F32
    )
    second_gelu, second_slope = gelu_and_slope(second)
    pred = lax.dot_general(second_gelu, out_w, across, precision=EXACT, preferred_element_type=F32)
    slope2 = second_slope * jnp.dot(
        pred - targets, out_w, precision=EXACT, preferred_element_type=F32
    )
    slope1 = first_slope * jnp.dot(
        slope2, mid_ref[...], precision=EXACT, preferred_element_type=F32
    )
    ours = lax.broadcasted_iota(jnp.int32, (16, 128), 0) // 4 == z_hi
    slope1 = jnp.where(ours, slope1, 0.0).astype(BF16)
    preds[z_hi] = jnp.where(ours, pred, 0.0)
    slope_in[z_hi] = slope1
    slope_copies = group_to(
        "z_hi", OTHERS, lambda step: (slope_in.at[z_hi], slope_in.at[z_hi]), slope_in.at[0:3]
    )
    pred_copies = group_to(
        "z_hi", OTHERS, lambda step: (preds.at[z_hi], preds.at[z_hi]), preds.at[0:3]
    )
    for k in range(4):
        for block in range(4):
            rows = slice(block * 256, block * 256 + 256)
            back[(z_hi - k + 4) % 4, block] = lax.dot_general(
                slope1, dense_w_ref[rows] if k == 0 else gathered[k - 1, rows], across,
                preferred_element_type=F32,
            )
    held_back = lax.dot_general(
        spread, back[...].reshape(256, 256), (((0,), (0,)), ((), ())), precision=EXACT,
        preferred_element_type=F32,
    )
    summed[...] = held_back.reshape(4, 64, 256)

    def turn(s, carry):
        spread_s = jnp.broadcast_to(summed[s].reshape(4, 1, 16, 256), (4, 4, 16, 256))
        cell = (spread_s.reshape(256, 256) * slope_at[s]).T.astype(BF16)
        for block in range(16):
            new = block % 2 * 8 + block // 2
            turned[s, new * 16 : new * 16 + 16] = cell[block * 16 : block * 16 + 16]
        return carry

    lax.fori_loop(0, 4, turn, 0)
    mine = pl.ds(pl.multiple_of(core * 128, 128), 128)
    theirs = pl.ds(pl.multiple_of(128 - core * 128, 128), 128)
    y_at = reserve(4)
    core_copies, x_first_copies = [], []
    lower[432:448] = jnp.zeros((16, 128), F32)

    def y_copy(block, from_y):
        return pltpu.make_async_remote_copy(
            src_ref=y_out.at[block], dst_ref=y_in.at[from_y],
            send_sem=send_sem.at[y_at + block], recv_sem=recv_sem.at[y_at + from_y],
            device_id=partner("y", block - y + 4), device_id_type=MESH,
        )

    def over_y(block):
        core_copies[block].wait_recv()
        rows = slice(block * 864, block * 864 + 864)
        total = kern[rows, mine].astype(F32) + core_in[block].astype(F32)

        @pl.when(y == block)
        def _():
            y_sum[0:432] = total[0:432]

        @pl.when(y != block)
        def _():
            y_out[block] = total[0:432].astype(BF16)
            y_copy(block, y).start()

        lower[0:432] = total[432:864]
        for hi in range(2):
            for to in range(4):
                start = (hi * 4 + to) * 54
                x_first[to, block, hi] = lower[start : start + 64].astype(BF16)
        x_first_copies.append(
            group_to(
                "x", OTHERS,
                lambda step: (x_first.at[(x + step) % 4, block], x_first_in.at[block, step - 1]),
                x_first_in.at[block],
            )
        )

    def hand_pooled():
        pool_copies.wait()
        order = one_hot(
            (64, 64),
            lambda r, c: (r // 16 == c // 4 % 4) & (r % 16 == c // 16 * 4 + c % 4),
            BF16,
        )
        rows = jnp.dot(order, pool_in[...].reshape(64, 256), preferred_element_type=F32)
        feat[core, z_lo] = rows.astype(BF16).reshape(4, 16, 256)
        return group_to(
            "z_lo", OCTET, lambda step: (feat.at[core, z_lo], feat.at[core, z_lo]), feat.at[core, 0:7]
        )

    def hand_slopes():
        slope_copies.wait()
        rows = (slope_in[0].astype(F32) + slope_in[1].astype(F32)) + (
            slope_in[2].astype(F32) + slope_in[3].astype(F32)
        )
        slopes[core, z_lo] = rows.astype(BF16)
        return group_to(
            "z_lo", OCTET,
            lambda step: (slopes.at[core, z_lo], slopes.at[core, z_lo]),
            slopes.at[core, 0:7],
        )

    for tap in range(9):
        a, b = tap // 3, tap % 3
        total = jnp.zeros((256, 384), F32)
        for s in range(4):
            total = total + jnp.dot(
                turned[s], wide[s, a : a + 4, b : b + 4].reshape(256, 384), preferred_element_type=F32
            )
        kern[tap * 384 : tap * 384 + 384] = total.T.astype(BF16)
        if tap in (2, 4, 6, 8):
            block = tap // 2 - 1
            rows = slice(block * 864, block * 864 + 864)
            core_copies.append(copy_to("core", 1, kern.at[rows, theirs], core_in.at[block]))
        if tap in (3, 5, 7):
            over_y(tap // 2 - 1)
        if tap == 5:
            feat_copies = hand_pooled()
    over_y(3)
    y_sum[432:448] = jnp.zeros((16, 128), F32)
    for block in range(4):

        @pl.when(y != block)
        def _(block=block):
            y_copy(block, block).wait()
            y_sum[0:432] = y_sum[0:432] + y_in[block].astype(F32)

    for hi in range(2):
        for to in range(4):
            start = (hi * 4 + to) * 54
            x_out[to, hi] = y_sum[start : start + 64].astype(BF16)
    x_copies = group_to(
        "x", OTHERS, lambda step: (x_out.at[(x + step) % 4], x_in.at[step - 1]), x_in.at[0:3]
    )
    lo_slopes = hand_slopes()
    for block in range(4):
        x_first_copies[block].wait()
        y_last[block] = (
            (x_first[x, block].astype(F32) + x_first_in[block, 0].astype(F32))
            + (x_first_in[block, 1].astype(F32) + x_first_in[block, 2].astype(F32))
        ).astype(BF16)
    y_last_copies = group_to(
        "y", OTHERS,
        lambda step: (y_last.at[(y + step) % 4], y_last_in.at[step - 1]),
        y_last_in.at[0:3],
    )
    x_copies.wait()
    upper_blocks = (x_out[x].astype(F32) + x_in[0].astype(F32)) + (
        x_in[1].astype(F32) + x_in[2].astype(F32)
    )
    y_last_copies.wait()
    lower_blocks = (y_last[y].astype(F32) + y_last_in[0].astype(F32)) + (
        y_last_in[1].astype(F32) + y_last_in[2].astype(F32)
    )
    for half, blocks in enumerate((upper_blocks, lower_blocks)):
        both = jnp.concatenate([blocks[0].T, blocks[1].T], axis=1)
        lo_out[:, half] = both.reshape(8, 16, 128).astype(BF16)
    turn_copies = group_to(
        "z_lo", OCTET, lambda step: (lo_out.at[(z_lo + step) % 8], lo_in.at[step - 1]), lo_in.at[0:7]
    )
    feat_copies.wait()
    lo_slopes.wait()
    pair = [
        copy_to("core", 1, feat.at[core], feat.at[core]),
        copy_to("core", 1, slopes.at[core], slopes.at[core]),
    ]
    turn_copies.wait()
    total = lo_out[z_lo].astype(F32)
    for step in range(7):
        total = total + lo_in[step].astype(F32)
    for hi in range(4):
        lanes = slice(hi % 2 * 64, hi % 2 * 64 + 64)
        hi_out[hi] = jnp.concatenate([total[hi // 2, 0:8, lanes], total[hi // 2, 8:16, lanes]], axis=1)
    hi_copies = group_to(
        "z_hi", OTHERS,
        lambda step: (hi_out.at[(z_hi + step) % 4], hi_in.at[step - 1]),
        hi_in.at[0:3],
    )
    for copy in pair:
        copy.wait()
    over = (((0,), (0,)), ((), ()))
    for block in range(4):
        sums = [
            lax.dot_general(
                feat[c, :, block].reshape(128, 256), slopes[c].reshape(128, 128), over,
                preferred_element_type=F32,
            )
            for c in range(2)
        ]
        dense_ref[block * 256 : block * 256 + 256] = sums[0] + sums[1]
    pred_copies.wait()
    sums = (preds[0] + preds[1]) + (preds[2] + preds[3])
    pred_ref[...] = jnp.concatenate([sums, jnp.zeros((112, 128), F32)], axis=0).T[0:4, 0:16]
    hi_copies.wait()
    total = (hi_out[z_hi] + hi_in[0]) + (hi_in[1] + hi_in[2])
    conv_ref[0:8] = total[:, 0:54]
    conv_ref[8:16] = total[:, 64:118]
    for copy in core_copies:
        copy.wait_send()
    assert used[0] == COPIES


def per_device(volume, conv_weight, dense_weight, mid_weight, out_weight, targets):
    vmem = pl.BlockSpec(memory_space=pltpu.VMEM)
    hbm = pl.BlockSpec(memory_space=pltpu.HBM)
    predictions, dense_grad, conv_grad = pl.pallas_call(
        kernel,
        name="conv_and_head",
        out_shape=(
            jax.ShapeDtypeStruct((4, 16), F32),
            jax.ShapeDtypeStruct((1024, 128), F32),
            jax.ShapeDtypeStruct((16, 54), F32),
        ),
        in_specs=[hbm] * 6,
        out_specs=(vmem,) * 3,
        scratch_shapes=[
            pltpu.VMEM((3456, 256), BF16),
            pltpu.VMEM((1024, 128), BF16),
            pltpu.VMEM((64, 128), F32),
            pltpu.VMEM((4, 64), F32),
            pltpu.VMEM((4, 16), F32),
            pltpu.VMEM((4, 6, 6, 16, 128), BF16),
            pltpu.VMEM((4, 6, 6, 16, 384), BF16),
            pltpu.VMEM((4, 256, 256), F32),
            pltpu.VMEM((4, 64, 256), F32),
            pltpu.VMEM((4, 4, 16, 256), BF16),
            pltpu.VMEM((4, 16, 256), BF16),
            pltpu.VMEM((4, 16, 256), BF16),
            pltpu.VMEM((2, 2, 4, 16, 128), BF16),
            pltpu.VMEM((3, 1024, 128), BF16),
            pltpu.VMEM((16, 16, 128), F32),
            pltpu.VMEM((4, 4, 16, 256), F32),
            pltpu.VMEM((4, 256, 256), BF16),
            pltpu.VMEM((4, 16, 128), F32),
            pltpu.VMEM((3456, 256), BF16),
            pltpu.VMEM((4, 864, 128), BF16),
            pltpu.VMEM((4, 432, 128), BF16),
            pltpu.VMEM((4, 432, 128), BF16),
            pltpu.VMEM((448, 128), F32),
            pltpu.VMEM((4, 2, 64, 128), BF16),
            pltpu.VMEM((3, 2, 64, 128), BF16),
            pltpu.VMEM((448, 128), F32),
            pltpu.VMEM((4, 4, 2, 64, 128), BF16),
            pltpu.VMEM((4, 3, 2, 64, 128), BF16),
            pltpu.VMEM((4, 2, 64, 128), BF16),
            pltpu.VMEM((3, 2, 64, 128), BF16),
            pltpu.VMEM((8, 2, 16, 128), BF16),
            pltpu.VMEM((7, 2, 16, 128), BF16),
            pltpu.VMEM((4, 8, 128), F32),
            pltpu.VMEM((3, 8, 128), F32),
            pltpu.VMEM((2, 8, 4, 16, 256), BF16),
            pltpu.VMEM((2, 8, 16, 128), BF16),
            pltpu.VMEM((4, 16, 128), BF16),
            pltpu.SemaphoreType.DMA((COPIES,)),
            pltpu.SemaphoreType.DMA((COPIES,)),
            pltpu.SemaphoreType.DMA((6,)),
        ],
        compiler_params=pltpu.CompilerParams(
            collective_id=0, has_side_effects=True, vmem_limit_bytes=40 * 2**20
        ),
    )(
        *(
            pltpu.with_memory_space_constraint(array, pltpu.HBM)
            for array in (
                volume.reshape(16, 4, 16, 128),
                conv_weight,
                dense_weight.reshape(1024, 128),
                mid_weight.T,
                out_weight.T,
                targets.T,
            )
        )
    )
    return predictions.T, dense_grad.reshape(dense_weight.shape), conv_grad.T


def solution(mesh):
    in_specs = (
        P("sample", "depth", "height", None, None),
        P(),
        P("depth", "height", None, None),
        P(),
        P(),
        P("sample", None),
    )
    out_specs = (
        P("sample", None),
        P("depth", "height", None, None),
        P(("depth", "height"), "sample"),
    )
    return jax.shard_map(
        per_device, mesh=mesh, in_specs=in_specs, out_specs=out_specs, check_vma=False
    )
```

```python
import jax
import jax.numpy as jnp
from jax import lax
from jax.experimental import pallas as pl
from jax.experimental.pallas import tpu as pltpu
from jax.sharding import PartitionSpec as P

F32 = jnp.float32
BF16 = jnp.bfloat16
MESH = pl.DeviceIdType.MESH
EXACT = lax.Precision.HIGHEST


def place():
    sample, depth, x = lax.axis_index("sample"), lax.axis_index("depth"), lax.axis_index("height")
    return sample // 2, sample % 2, depth // 4, depth % 4, x


def partner(kind, step):
    z_lo, core, y, z_hi, x = place()
    if kind == "z_lo":
        z_lo = (z_lo + step) % 8
    elif kind == "z_four":
        z_lo = (z_lo // 4) * 4 + (z_lo + step) % 4
    elif kind == "core":
        core = (core + step) % 2
    elif kind == "y":
        y = (y + step) % 4
    elif kind == "z_hi":
        z_hi = (z_hi + step) % 4
    elif kind == "x":
        x = (x + step) % 4
    else:
        y, x = (y + step[0]) % 4, (x + step[1]) % 4
    return (z_lo * 2 + core, y * 4 + z_hi, x)


AROUND = [(dy, dx) for dy in (2, 1, 3, 0) for dx in (2, 1, 3, 0) if (dy, dx) != (0, 0)]
OTHERS = (2, 1, 3)
OCTET = range(1, 8)
CORNERS = [("corner", (dy, dx)) for dy in (1, 3) for dx in (1, 3)]
PARTNERS = [("core", 1)] + [("z_hi", 1), ("z_hi", 3)] + [("z_lo", step) for step in OCTET] + [("corner", step) for step in AROUND]
COPIES = 41


def gelu_and_slope(value):
    rate = 0.7978845608028654
    square = value * value
    bend = jnp.tanh(rate * (value + 0.044715 * value * square))
    half = 0.5 * (1.0 + bend)
    slope = half + 0.5 * value * (1.0 - bend * bend) * (rate * (1.0 + 3 * 0.044715 * square))
    return value * half, slope


def one_hot(shape, test, kind, weight=1.0):
    row = lax.broadcasted_iota(jnp.int32, shape, 0)
    column = lax.broadcasted_iota(jnp.int32, shape, 1)
    return jnp.where(test(row, column), weight, 0.0).astype(kind)


def kernel(
    vol_ref, weight_hbm, dense_w_hbm, mid_hbm, out_w_hbm, targets_hbm,
    pred_ref, dense_ref, conv_ref,
    weight_ref, dense_w_ref, mid_ref, out_w_ref, targets_ref,
    ext, wide, slope_at, summed, pool, pool_out, pool_in, vol_relay, gathered, held, back, turned, preds,
    kern, core_in, y_out, y_in, y_sum, x_out, x_in,
    lower, x_first, x_first_in, y_last, y_last_in, lo_out, lo_in, hi_out, hi_in,
    feat, slopes, slope_in,
    send_sem, recv_sem, local_sem,
):
    z_lo, core, y, z_hi, x = place()
    used = [0]

    def reserve(count):
        used[0] += count
        assert used[0] <= COPIES
        return used[0] - count

    def copy_to(kind, step, src, dst):
        at = reserve(1)
        copy = pltpu.make_async_remote_copy(
            src_ref=src, dst_ref=dst, send_sem=send_sem.at[at], recv_sem=recv_sem.at[at],
            device_id=partner(kind, step), device_id_type=MESH,
        )
        copy.start()
        return copy

    def group_to(kind, steps, pair_of, span):
        at = reserve(1)
        sems = dict(send_sem=send_sem.at[at], recv_sem=recv_sem.at[at], device_id_type=MESH)
        for step in steps:
            src, dst = pair_of(step)
            pltpu.make_async_remote_copy(
                src_ref=src, dst_ref=dst, device_id=partner(kind, step), **sems
            ).start()
        return pltpu.make_async_remote_copy(
            src_ref=span, dst_ref=span, device_id=partner(kind, steps[0]), **sems
        )

    barrier = pltpu.get_barrier_semaphore()
    for kind, step in PARTNERS:
        pl.semaphore_signal(barrier, inc=1, device_id=partner(kind, step), device_id_type=MESH)
    local = [
        (vol_ref.at[pl.ds(z_hi * 4, 4)], ext.at[:, 1 + z_hi, 1:5]),
        (dense_w_hbm, dense_w_ref),
        (weight_hbm, weight_ref),
        (mid_hbm, mid_ref),
        (out_w_hbm, out_w_ref),
        (targets_hbm, targets_ref),
    ]
    local = [pltpu.make_async_copy(src, dst, local_sem.at[at]) for at, (src, dst) in enumerate(local)]
    for copy in local:
        copy.start()
    pl.semaphore_wait(barrier, len(PARTNERS))

    far = (z_hi + 2) % 4
    ways = ((0, 1), (1, 3))
    vol_on = [
        copy_to("z_hi", step, vol_ref.at[pl.ds(far * 4 + 2 * way, 2)], vol_relay.at[way])
        for way, step in ways
    ]
    vol_copies = [
        copy_to("z_hi", step, vol_ref.at[pl.ds((z_hi + step) % 4 * 4, 4)], ext.at[:, 1 + z_hi, 1:5])
        for way, step in ways
    ]
    start = pl.multiple_of(core * 512 + (z_lo % 4) * 128, 128)
    share = pl.ds(start, 128)
    for (way, step), copy in zip(ways, vol_on):
        copy.wait_recv()
        vol_copies.append(
            copy_to(
                "z_hi", step, vol_relay.at[way],
                ext.at[2 * way : 2 * way + 2, 1 + (z_hi + 4 - step) % 4, 1:5],
            )
        )
    hi_weights = group_to(
        "z_hi", OTHERS,
        lambda step: (dense_w_hbm.at[share], gathered.at[step - 1, share]),
        gathered.at[:, share],
    )
    for copy in local:
        copy.wait()
    for copy in vol_copies:
        copy.wait_recv()
    y_halo = [
        copy_to("y", 1, ext.at[:, 4, 1:5], ext.at[:, 0, 1:5]),
        copy_to("y", 3, ext.at[:, 1, 1:5], ext.at[:, 5, 1:5]),
    ]
    x_halo = [
        copy_to("x", 1, ext.at[:, 1:5, 4], ext.at[:, 1:5, 0]),
        copy_to("x", 3, ext.at[:, 1:5, 1], ext.at[:, 1:5, 5]),
    ]
    for kind, (dy, dx) in CORNERS:
        src = ext.at[:, 4 if dy == 1 else 1, 4 if dx == 1 else 1]
        dst = ext.at[:, 0 if dy == 1 else 5, 0 if dx == 1 else 5]
        x_halo.append(copy_to(kind, (dy, dx), src, dst))
    hi_weights.wait()
    lo_weights = group_to(
        "z_four", (1, 2, 3),
        lambda step: (gathered.at[:, share], gathered.at[:, share]),
        gathered.at[:, 0:384],
    )
    for copy in x_halo + y_halo:
        copy.wait()
    for copy in vol_on + vol_copies:
        copy.wait_send()

    @pl.when(y == 0)
    def _():
        ext[:, 0] = jnp.zeros((4, 6, 16, 128), BF16)

    @pl.when(y == 3)
    def _():
        ext[:, 5] = jnp.zeros((4, 6, 16, 128), BF16)

    @pl.when(x == 0)
    def _():
        ext[:, :, 0] = jnp.zeros((4, 6, 16, 128), BF16)

    @pl.when(x == 3)
    def _():
        ext[:, :, 5] = jnp.zeros((4, 6, 16, 128), BF16)

    def forward(s, carry):
        cells = ext[s].reshape(36, 16, 128).astype(F32)
        edge = jnp.zeros((36, 1, 128), F32)
        wide[s, :, :, :, 0:128] = (
            jnp.concatenate([edge, cells[:, :15]], axis=1).astype(BF16).reshape(6, 6, 16, 128)
        )
        wide[s, :, :, :, 128:256] = ext[s]
        wide[s, :, :, :, 256:384] = (
            jnp.concatenate([cells[:, 1:], edge], axis=1).astype(BF16).reshape(6, 6, 16, 128)
        )
        pre = jnp.zeros((256, 256), F32)
        for tap in range(9):
            a, b = tap // 3, tap % 3
            pre = pre + jnp.dot(
                wide[s, a : a + 4, b : b + 4].reshape(256, 384),
                weight_ref[tap * 384 : tap * 384 + 384],
                preferred_element_type=F32,
            )
        active, slope = gelu_and_slope(pre)
        slope_at[s] = slope
        summed[s] = jnp.sum(active.reshape(4, 4, 16, 256), axis=1).reshape(64, 256)
        return carry

    lax.fori_loop(0, 4, forward, 0)
    lo_weights.wait()
    half_rows = pl.ds(pl.multiple_of(core * 512, 512), 512)
    pair_weights = copy_to("core", 1, gathered.at[:, half_rows], gathered.at[:, half_rows])

    spread = one_hot(
        (256, 256),
        lambda r, c: (r // 64 == c // 16 % 4)
        & (r // 16 % 4 == c % 16 // 4)
        & (r % 16 == z_hi * 4 + c // 64),
        F32,
        1.0 / 16,
    )
    pooled = jnp.dot(
        spread, summed[...].reshape(256, 256), precision=EXACT, preferred_element_type=F32
    ).astype(BF16)
    pool[...] = pooled.reshape(4, 4, 16, 256)
    order = one_hot(
        (64, 256),
        lambda r, c: (r // 16 == c // 64)
        & (r // 4 % 4 == c // 16 % 4)
        & (z_hi * 4 + r % 4 == c % 16),
        BF16,
    )
    pool_out[...] = (
        jnp.dot(order, pooled, preferred_element_type=F32).astype(BF16).reshape(4, 16, 256)
    )
    pool_in[z_hi] = pool_out[z_hi]
    pool_copies = group_to(
        "z_hi", OTHERS,
        lambda step: (pool_out.at[(z_hi + step) % 4], pool_in.at[z_hi]),
        pool_in.at[0:3],
    )
    total = jnp.zeros((16, 128), F32)
    for k in range(4):
        if k == 1:
            pair_weights.wait()
        for block in range(4):
            rows = slice(block * 256, block * 256 + 256)
            total = total + jnp.dot(
                pool[(z_hi - k + 4) % 4, block],
                dense_w_ref[rows] if k == 0 else gathered[k - 1, rows],
                preferred_element_type=F32,
            )
    here = y * 4 + x
    held[here] = total
    group_to("corner", AROUND, lambda step: (held.at[here], held.at[here]), held.at[0:15]).wait()
    total = held[0]
    for at in range(1, 16):
        total = total + held[at]
    first = total
    out_w = jnp.concatenate([out_w_ref[...], jnp.zeros((124, 64), F32)], axis=0)
    across = (((1,), (1,)), ((), ()))
    targets = lax.dot_general(
        one_hot((16, 16), lambda r, c: r == c, F32),
        jnp.concatenate([targets_ref[...], jnp.zeros((124, 16), F32)], axis=0),
        across, precision=EXACT, preferred_element_type=F32,
    )
    first_gelu, first_slope = gelu_and_slope(first)
    second = lax.dot_general(
        first_gelu, mid_ref[...], across, precision=EXACT, preferred_element_type=F32
    )
    second_gelu, second_slope = gelu_and_slope(second)
    pred = lax.dot_general(second_gelu, out_w, across, precision=EXACT, preferred_element_type=F32)
    slope2 = second_slope * jnp.dot(
        pred - targets, out_w, precision=EXACT, preferred_element_type=F32
    )
    slope1 = first_slope * jnp.dot(
        slope2, mid_ref[...], precision=EXACT, preferred_element_type=F32
    )
    ours = lax.broadcasted_iota(jnp.int32, (16, 128), 0) // 4 == z_hi
    slope1 = jnp.where(ours, slope1, 0.0).astype(BF16)
    preds[z_hi] = jnp.where(ours, pred, 0.0)
    slope_in[z_hi] = slope1
    slope_copies = group_to(
        "z_hi", OTHERS, lambda step: (slope_in.at[z_hi], slope_in.at[z_hi]), slope_in.at[0:3]
    )
    pred_copies = group_to(
        "z_hi", OTHERS, lambda step: (preds.at[z_hi], preds.at[z_hi]), preds.at[0:3]
    )
    for k in range(4):
        for block in range(4):
            rows = slice(block * 256, block * 256 + 256)
            back[(z_hi - k + 4) % 4, block] = lax.dot_general(
                slope1, dense_w_ref[rows] if k == 0 else gathered[k - 1, rows], across,
                preferred_element_type=F32,
            )
    held_back = lax.dot_general(
        spread, back[...].reshape(256, 256), (((0,), (0,)), ((), ())), precision=EXACT,
        preferred_element_type=F32,
    )
    summed[...] = held_back.reshape(4, 64, 256)

    def turn(s, carry):
        spread_s = jnp.broadcast_to(summed[s].reshape(4, 1, 16, 256), (4, 4, 16, 256))
        cell = (spread_s.reshape(256, 256) * slope_at[s]).T.astype(BF16)
        for block in range(16):
            new = block % 2 * 8 + block // 2
            turned[s, new * 16 : new * 16 + 16] = cell[block * 16 : block * 16 + 16]
        return carry

    lax.fori_loop(0, 4, turn, 0)
    mine = pl.ds(pl.multiple_of(core * 128, 128), 128)
    theirs = pl.ds(pl.multiple_of(128 - core * 128, 128), 128)
    y_at = reserve(4)
    core_copies, x_first_copies = [], []
    lower[432:448] = jnp.zeros((16, 128), F32)

    def y_copy(block, from_y):
        return pltpu.make_async_remote_copy(
            src_ref=y_out.at[block], dst_ref=y_in.at[from_y],
            send_sem=send_sem.at[y_at + block], recv_sem=recv_sem.at[y_at + from_y],
            device_id=partner("y", block - y + 4), device_id_type=MESH,
        )

    def over_y(block):
        core_copies[block].wait_recv()
        rows = slice(block * 864, block * 864 + 864)
        total = kern[rows, mine].astype(F32) + core_in[block].astype(F32)

        @pl.when(y == block)
        def _():
            y_sum[0:432] = total[0:432]

        @pl.when(y != block)
        def _():
            y_out[block] = total[0:432].astype(BF16)
            y_copy(block, y).start()

        lower[0:432] = total[432:864]
        for hi in range(2):
            for to in range(4):
                start = (hi * 4 + to) * 54
                x_first[to, block, hi] = lower[start : start + 64].astype(BF16)
        x_first_copies.append(
            group_to(
                "x", OTHERS,
                lambda step: (x_first.at[(x + step) % 4, block], x_first_in.at[block, step - 1]),
                x_first_in.at[block],
            )
        )

    def hand_pooled():
        pool_copies.wait()
        order = one_hot(
            (64, 64),
            lambda r, c: (r // 16 == c // 4 % 4) & (r % 16 == c // 16 * 4 + c % 4),
            BF16,
        )
        rows = jnp.dot(order, pool_in[...].reshape(64, 256), preferred_element_type=F32)
        feat[core, z_lo] = rows.astype(BF16).reshape(4, 16, 256)
        return group_to(
            "z_lo", OCTET, lambda step: (feat.at[core, z_lo], feat.at[core, z_lo]), feat.at[core, 0:7]
        )

    def hand_slopes():
        slope_copies.wait()
        rows = (slope_in[0].astype(F32) + slope_in[1].astype(F32)) + (
            slope_in[2].astype(F32) + slope_in[3].astype(F32)
        )
        slopes[core, z_lo] = rows.astype(BF16)
        return group_to(
            "z_lo", OCTET,
            lambda step: (slopes.at[core, z_lo], slopes.at[core, z_lo]),
            slopes.at[core, 0:7],
        )

    for tap in range(9):
        a, b = tap // 3, tap % 3
        total = jnp.zeros((256, 384), F32)
        for s in range(4):
            total = total + jnp.dot(
                turned[s], wide[s, a : a + 4, b : b + 4].reshape(256, 384), preferred_element_type=F32
            )
        kern[tap * 384 : tap * 384 + 384] = total.T.astype(BF16)
        if tap in (2, 4, 6, 8):
            block = tap // 2 - 1
            rows = slice(block * 864, block * 864 + 864)
            core_copies.append(copy_to("core", 1, kern.at[rows, theirs], core_in.at[block]))
        if tap in (3, 5, 7):
            over_y(tap // 2 - 1)
        if tap == 5:
            feat_copies = hand_pooled()
    over_y(3)
    y_sum[432:448] = jnp.zeros((16, 128), F32)
    for block in range(4):

        @pl.when(y != block)
        def _(block=block):
            y_copy(block, block).wait()
            y_sum[0:432] = y_sum[0:432] + y_in[block].astype(F32)

    for hi in range(2):
        for to in range(4):
            start = (hi * 4 + to) * 54
            x_out[to, hi] = y_sum[start : start + 64].astype(BF16)
    x_copies = group_to(
        "x", OTHERS, lambda step: (x_out.at[(x + step) % 4], x_in.at[step - 1]), x_in.at[0:3]
    )
    lo_slopes = hand_slopes()
    for block in range(4):
        x_first_copies[block].wait()
        y_last[block] = (
            (x_first[x, block].astype(F32) + x_first_in[block, 0].astype(F32))
            + (x_first_in[block, 1].astype(F32) + x_first_in[block, 2].astype(F32))
        ).astype(BF16)
    y_last_copies = group_to(
        "y", OTHERS,
        lambda step: (y_last.at[(y + step) % 4], y_last_in.at[step - 1]),
        y_last_in.at[0:3],
    )
    x_copies.wait()
    upper_blocks = (x_out[x].astype(F32) + x_in[0].astype(F32)) + (
        x_in[1].astype(F32) + x_in[2].astype(F32)
    )
    y_last_copies.wait()
    lower_blocks = (y_last[y].astype(F32) + y_last_in[0].astype(F32)) + (
        y_last_in[1].astype(F32) + y_last_in[2].astype(F32)
    )
    for half, blocks in enumerate((upper_blocks, lower_blocks)):
        both = jnp.concatenate([blocks[0].T, blocks[1].T], axis=1)
        lo_out[:, half] = both.reshape(8, 16, 128).astype(BF16)
    turn_copies = group_to(
        "z_lo", OCTET, lambda step: (lo_out.at[(z_lo + step) % 8], lo_in.at[step - 1]), lo_in.at[0:7]
    )
    turn_copies.wait()
    total = lo_out[z_lo].astype(F32)
    for step in range(7):
        total = total + lo_in[step].astype(F32)
    for hi in range(4):
        lanes = slice(hi % 2 * 64, hi % 2 * 64 + 64)
        hi_out[hi] = jnp.concatenate([total[hi // 2, 0:8, lanes], total[hi // 2, 8:16, lanes]], axis=1)
    hi_copies = group_to(
        "z_hi", OTHERS,
        lambda step: (hi_out.at[(z_hi + step) % 4], hi_in.at[step - 1]),
        hi_in.at[0:3],
    )
    feat_copies.wait()
    lo_slopes.wait()
    pair = [
        copy_to("core", 1, feat.at[core], feat.at[core]),
        copy_to("core", 1, slopes.at[core], slopes.at[core]),
    ]
    for copy in pair:
        copy.wait()
    over = (((0,), (0,)), ((), ()))
    for block in range(4):
        sums = [
            lax.dot_general(
                feat[c, :, block].reshape(128, 256), slopes[c].reshape(128, 128), over,
                preferred_element_type=F32,
            )
            for c in range(2)
        ]
        dense_ref[block * 256 : block * 256 + 256] = sums[0] + sums[1]
    pred_copies.wait()
    sums = (preds[0] + preds[1]) + (preds[2] + preds[3])
    pred_ref[...] = jnp.concatenate([sums, jnp.zeros((112, 128), F32)], axis=0).T[0:4, 0:16]
    hi_copies.wait()
    total = (hi_out[z_hi] + hi_in[0]) + (hi_in[1] + hi_in[2])
    conv_ref[0:8] = total[:, 0:54]
    conv_ref[8:16] = total[:, 64:118]
    for copy in core_copies:
        copy.wait_send()
    assert used[0] == COPIES


def per_device(volume, conv_weight, dense_weight, mid_weight, out_weight, targets):
    vmem = pl.BlockSpec(memory_space=pltpu.VMEM)
    hbm = pl.BlockSpec(memory_space=pltpu.HBM)
    predictions, dense_grad, conv_grad = pl.pallas_call(
        kernel,
        name="conv_and_head",
        out_shape=(
            jax.ShapeDtypeStruct((4, 16), F32),
            jax.ShapeDtypeStruct((1024, 128), F32),
            jax.ShapeDtypeStruct((16, 54), F32),
        ),
        in_specs=[hbm] * 6,
        out_specs=(vmem,) * 3,
        scratch_shapes=[
            pltpu.VMEM((3456, 256), BF16),
            pltpu.VMEM((1024, 128), BF16),
            pltpu.VMEM((64, 128), F32),
            pltpu.VMEM((4, 64), F32),
            pltpu.VMEM((4, 16), F32),
            pltpu.VMEM((4, 6, 6, 16, 128), BF16),
            pltpu.VMEM((4, 6, 6, 16, 384), BF16),
            pltpu.VMEM((4, 256, 256), F32),
            pltpu.VMEM((4, 64, 256), F32),
            pltpu.VMEM((4, 4, 16, 256), BF16),
            pltpu.VMEM((4, 16, 256), BF16),
            pltpu.VMEM((4, 16, 256), BF16),
            pltpu.VMEM((2, 2, 4, 16, 128), BF16),
            pltpu.VMEM((3, 1024, 128), BF16),
            pltpu.VMEM((16, 16, 128), F32),
            pltpu.VMEM((4, 4, 16, 256), F32),
            pltpu.VMEM((4, 256, 256), BF16),
            pltpu.VMEM((4, 16, 128), F32),
            pltpu.VMEM((3456, 256), BF16),
            pltpu.VMEM((4, 864, 128), BF16),
            pltpu.VMEM((4, 432, 128), BF16),
            pltpu.VMEM((4, 432, 128), BF16),
            pltpu.VMEM((448, 128), F32),
            pltpu.VMEM((4, 2, 64, 128), BF16),
            pltpu.VMEM((3, 2, 64, 128), BF16),
            pltpu.VMEM((448, 128), F32),
            pltpu.VMEM((4, 4, 2, 64, 128), BF16),
            pltpu.VMEM((4, 3, 2, 64, 128), BF16),
            pltpu.VMEM((4, 2, 64, 128), BF16),
            pltpu.VMEM((3, 2, 64, 128), BF16),
            pltpu.VMEM((8, 2, 16, 128), BF16),
            pltpu.VMEM((7, 2, 16, 128), BF16),
            pltpu.VMEM((4, 8, 128), F32),
            pltpu.VMEM((3, 8, 128), F32),
            pltpu.VMEM((2, 8, 4, 16, 256), BF16),
            pltpu.VMEM((2, 8, 16, 128), BF16),
            pltpu.VMEM((4, 16, 128), BF16),
            pltpu.SemaphoreType.DMA((COPIES,)),
            pltpu.SemaphoreType.DMA((COPIES,)),
            pltpu.SemaphoreType.DMA((6,)),
        ],
        compiler_params=pltpu.CompilerParams(
            collective_id=0, has_side_effects=True, vmem_limit_bytes=40 * 2**20
        ),
    )(
        *(
            pltpu.with_memory_space_constraint(array, pltpu.HBM)
            for array in (
                volume.reshape(16, 4, 16, 128),
                conv_weight,
                dense_weight.reshape(1024, 128),
                mid_weight.T,
                out_weight.T,
                targets.T,
            )
        )
    )
    return predictions.T, dense_grad.reshape(dense_weight.shape), conv_grad.T


def solution(mesh):
    in_specs = (
        P("sample", "depth", "height", None, None),
        P(),
        P("depth", "height", None, None),
        P(),
        P(),
        P("sample", None),
    )
    out_specs = (
        P("sample", None),
        P("depth", "height", None, None),
        P(("depth", "height"), "sample"),
    )
    return jax.shard_map(
        per_device, mesh=mesh, in_specs=in_specs, out_specs=out_specs, check_vma=False
    )
```
